32 devices in a mesh: tm: 4 (over y, core), space: 8 (over z, x).
Axes of the slice: x: 2, y: 2, z: 4, core: 2. Of those that a mesh axis runs over, the one named last changes fastest.
Arguments:
- background: bfloat16 [65536, 64], P('space'), may hold values from -4 to 4
- probe: bfloat16 [64, 32], replicated, may hold values from -0.75 to 0.75
- member_scale: float32 [64], replicated, may hold values from 0.5 to 2
- decay: float32 [12, 32], P('tm'), may hold values from 0.36 to 1
- inflation: float32 [12], P('tm'), may hold values from 0.05 to 0.5
- obs_owner: int32 [12, 16384, 1], P('tm', 'space'), may hold values from 0 to 7; in each aligned block of 2048 rows (0 to 2047, 2048 to 4095, ..., all dimensions but the last counted through in order) at most 512 rows name the same one
- obs_offset: int32 [12, 16384], P('tm', 'space'), may hold values from 0 to 8191
- obs_value: float32 [12, 16384], P('tm', 'space'), may hold values from -360 to 360
- obs_weight: float32 [12, 16384], P('tm', 'space'), may hold values from 0.0002 to 0.002
Outputs:
- smooth_mean: float32 [12, 65536], P('tm', 'space')
- smooth_spread: float32 [12, 65536], P('tm', 'space')
The draws below stay inside these ranges and needn't reach their ends.
Inputs may be any that keep to these rules, and one draw needn't show every extreme that they name: `obs_owner`: of the 2048 observations that one reader holds for one day, at most 512 name the same owner, and 512 is reached.
All inputs are finite; a program needn't handle non-finite values.
Results may differ from the reference program's by a relative error of at most 0.0029.
Values sent between devices are 32-bit elements; how exact they have to be, the bound alone decides.
A program may use at most 64 MiB of HBM per device.

```python
import math
import jax
import jax.numpy as jnp
import numpy as np
from jax import lax

RANK = 32
MEMBERS = 64
CELLS_DEV = 8192
OBS_DEV = 2048
CELLS = 65536
DAILY_STEPS = 12
CAP = 512
N_SPACE = 8


def draw_decay(key, part):
    random_key_list = jax.random.split(key, 4)
    slow_share = 0.5
    slow_mask = jax.random.uniform(random_key_list[0], (RANK,)) < slow_share
    jitter = jax.random.uniform(random_key_list[1], (DAILY_STEPS, RANK), minval=0.5, maxval=1.5)
    fast_scale = jax.random.uniform(random_key_list[2], (RANK,), minval=3.0, maxval=9.0)
    slow_day = jnp.exp(jitter * (math.log(0.5) / DAILY_STEPS))
    fast_day = jnp.exp(-jitter / fast_scale[None, :])
    surge_day_list = jax.random.randint(random_key_list[3], (3,), 0, DAILY_STEPS)
    surge_row_list = jnp.any(jnp.arange(DAILY_STEPS)[:, None] == surge_day_list[None, :], axis=1)
    selected_entries = jnp.where(slow_mask[None, :], slow_day, fast_day)
    return (selected_entries * jnp.where(surge_row_list, 0.6, 1.0)[:, None]).astype(jnp.float32)


def draw_background(key, part):
    key_list = jax.random.split(jax.random.fold_in(key, 17), 3)
    strength = 0.7
    own_part = jnp.clip(jax.random.normal(key_list[0], (CELLS, MEMBERS), jnp.float32), -6.0, 6.0)
    cell_factor = jnp.clip(jax.random.normal(key_list[1], (4, CELLS), jnp.float32), -4.0, 4.0)
    member_factor = jnp.clip(jax.random.normal(key_list[2], (4, MEMBERS), jnp.float32), -4.0, 4.0)
    shared_part = cell_factor[0][:, None] * member_factor[0][None, :]
    shared_part = shared_part + cell_factor[1][:, None] * member_factor[1][None, :]
    shared_part = shared_part + cell_factor[2][:, None] * member_factor[2][None, :]
    shared_part = shared_part + cell_factor[3][:, None] * member_factor[3][None, :]
    norm_factor = 1.0 / math.sqrt(MEMBERS * (1.0 + 4.0 * strength * strength))
    return ((own_part + strength * shared_part) * norm_factor).astype(jnp.bfloat16)


def touch_ends(array, key, least, largest):
    longest = array.shape.index(max(array.shape))
    spots = []
    for shift in (0, 1):
        where = [jax.random.randint(jax.random.fold_in(key, axis), (), 0, length) for axis, length in enumerate(array.shape)]
        where[longest] = (where[longest] + shift) % array.shape[longest]
        spots.append(tuple(where))
    return array.at[spots[0]].set(least).at[spots[1]].set(largest)


def steps_of(own_key, shape, pieces, smallest, top_value):
    level = 1.0
    for dim, parts in pieces:
        draws = jax.random.uniform(jax.random.fold_in(jax.random.fold_in(own_key, 6), dim), (parts,), jnp.float32, smallest / len(pieces), top_value / len(pieces))
        level = level * jnp.repeat(jnp.exp(draws), shape[dim] // parts).reshape((-1,) + (1,) * (len(shape) - 1 - dim))
    return level


def deal_out(stream_key, own, number, rows, amount, top, reach, skew):
    ranking = jax.random.permutation(stream_key, amount)
    crowded, common = shares(amount, rows * top, reach, skew, True), shares(amount, rows * top, reach, skew, False)
    places = jnp.arange(amount)

    def named(sizes, turn):
        used = int((sizes > 0).sum())
        fixed = max(1, used // 4)
        shifted = fixed + (places - fixed + turn * (used - fixed)) % max(1, amount - fixed)
        return jnp.zeros((amount,), jnp.int32).at[ranking[jnp.where(places < fixed, places, shifted)]].set(jnp.asarray(sizes, jnp.int32))

    sizes = jnp.where(number % 4 == 0, named(crowded, number // 4), named(common, number - number // 4 - 1))
    mixed = jax.random.permutation(jax.random.fold_in(own, 3), amount)
    donor, sink = mixed[0:amount // 2 * 2:2], mixed[1:amount // 2 * 2:2]
    room = jnp.minimum(sizes[donor] - 1, reach - sizes[sink]) // 2
    room = jnp.where((donor == ranking[0]) | (sink == ranking[0]) | (sizes[sink] == 0), 0, jnp.maximum(room, 0))
    shifted = jax.random.randint(jax.random.fold_in(own, 4), (amount // 2,), 0, 1 << 20) % (room + 1)
    sizes = sizes.at[donor].add(-shifted).at[sink].add(shifted)
    items = jnp.searchsorted(jnp.cumsum(sizes), jnp.arange(rows * top), side="right").astype(jnp.int32)
    grid = items.reshape(top, rows).T
    grid = grid[jax.random.permutation(jax.random.fold_in(own, 1), rows)]
    turn = jax.random.randint(jax.random.fold_in(own, 2), (rows, 1), 0, top)
    return jnp.take_along_axis(grid, (jnp.arange(top)[None, :] + turn) % top, axis=1)


def shares(amount, total, most, skew, full):
    weights = [(1 << 20) // math.isqrt(rank ** skew) + 1 for rank in range(1, amount + 1)]
    largest = most if full else min(most, max(-(-total // amount), total * weights[0] // sum(weights)))
    least = 1 if total - largest >= amount - 1 else 0
    given, spare = [largest] + [least] * (amount - 1), total - largest - least * (amount - 1)
    while spare > 0:
        movable = [i for i in range(1, amount) if given[i] < largest] or [i for i in range(1, amount) if given[i] < most]
        pool, remaining = sum([weights[i] for i in movable]), spare
        for i in movable:
            extra = min(most - given[i], max(1, remaining * weights[i] // pool), spare)
            given[i] = given[i] + extra
            spare = spare - extra
    return np.array(given)


def scatter_about(own_key, extent, deviation, reach, cuts=(), kind=jnp.bfloat16):
    values = deviation * jax.random.normal(own_key, extent, jnp.float32)
    if cuts:
        values = values * steps_of(own_key, extent, cuts, -0.22, 0.18)
    return jnp.clip(values, -reach, reach).astype(kind)


def setup_inputs(seed: int = 0) -> dict:
    splits = jax.random.split(jax.random.key(seed), 10)
    background = draw_background(jax.random.fold_in(splits[9], 71), 0)
    probe = scatter_about(splits[1], (MEMBERS, RANK), MEMBERS ** -0.5, 0.75)
    member_scale = jnp.clip(jnp.exp(jax.random.uniform(splits[2], (MEMBERS,), jnp.float32, math.log(0.5), math.log(2.0))), 0.5, 2.0)
    decay = draw_decay(jax.random.fold_in(splits[9], 71), 0)
    inflation = jnp.clip(jnp.exp(math.log(0.5) - 2.3025851 * jax.random.uniform(splits[4], (DAILY_STEPS,), jnp.float32) ** steps_of(splits[4], (DAILY_STEPS,), ((0, 4),), -0.2, 0.2)), 0.05, 0.5)
    obs_owner_keys = jax.random.split(jax.random.fold_in(splits[5], 1), DAILY_STEPS * (OBS_DEV * N_SPACE) // OBS_DEV)
    obs_owner_turns = jax.random.permutation(jax.random.fold_in(splits[5], 3), DAILY_STEPS * (OBS_DEV * N_SPACE) // OBS_DEV)
    obs_owner = jax.vmap(lambda own, number: deal_out(jax.random.fold_in(splits[5], 2), own, number, OBS_DEV, N_SPACE, 1, CAP, 2))(obs_owner_keys, obs_owner_turns).reshape((DAILY_STEPS, OBS_DEV * N_SPACE, 1))
    obs_offset = touch_ends(jax.random.randint(splits[6], (DAILY_STEPS, OBS_DEV * N_SPACE), 0, CELLS_DEV), jax.random.fold_in(splits[6], 1), 0, CELLS_DEV - 1).astype(jnp.int32)
    obs_value = scatter_about(splits[7], (DAILY_STEPS, OBS_DEV * N_SPACE), 60.0, 360.0, ((0, 4), (1, 8)), jnp.float32)
    obs_weight = jnp.clip(jnp.exp(math.log(0.002) - 2.3025852 * jax.random.uniform(splits[8], (DAILY_STEPS, OBS_DEV * N_SPACE), jnp.float32) ** steps_of(splits[8], (DAILY_STEPS, OBS_DEV * N_SPACE), ((0, 4), (1, 8)), -0.2, 0.2)), 0.0002, 0.002)
    return dict(background=background, probe=probe, member_scale=member_scale, decay=decay, inflation=inflation, obs_owner=obs_owner, obs_offset=obs_offset, obs_value=obs_value, obs_weight=obs_weight)


HIGHEST = lax.Precision.HIGHEST

def matmul_high(left_mat, right_mat):
    return jnp.matmul(left_mat, right_mat, precision=HIGHEST)

def matvec_high(matrix, vector):
    return matmul_high(matrix, vector[..., None])[..., 0]

def flip_last(matrix):
    return jnp.swapaxes(matrix, -1, -2)

def symmetric(matrix):
    return 0.5 * (matrix + flip_last(matrix))

def spd_solve(matrix, right_side):
    lower_chol = jnp.linalg.cholesky(matrix)
    middle = lax.linalg.triangular_solve(lower_chol, right_side, left_side=True, lower=True)
    return lax.linalg.triangular_solve(lower_chol, middle, left_side=True, lower=True, transpose_a=True)

def spd_inverse(matrix):
    identity_mat = jnp.broadcast_to(jnp.eye(matrix.shape[-1], dtype=jnp.float32), matrix.shape)
    return spd_solve(matrix, identity_mat)

def reference(background, probe, member_scale, decay, inflation, obs_owner, obs_offset, obs_value, obs_weight):
    scaled_probe = (probe.astype(jnp.float32) * member_scale[:, None]).astype(jnp.bfloat16)
    field_basis = jnp.dot(background.astype(jnp.float32), scaled_probe.astype(jnp.float32), preferred_element_type=jnp.float32)
    member_gram = jnp.dot(background.T.astype(jnp.float32), background.astype(jnp.float32), preferred_element_type=jnp.float32)
    probe_wide = scaled_probe.astype(jnp.float32)
    core_gram = matmul_high(matmul_high(probe_wide.T, member_gram), probe_wide)
    lower_chol = jnp.linalg.cholesky(core_gram)
    lower_inv = lax.linalg.triangular_solve(lower_chol, jnp.eye(RANK, dtype=jnp.float32), left_side=True, lower=True)
    basis = matmul_high(field_basis, lower_inv.T)
    projected = matmul_high(lower_inv, matmul_high(probe_wide.T, member_gram))
    prior_cov = matmul_high(projected * (member_scale * member_scale)[None, :], projected.T)
    cells = (obs_owner[:, :, 0] * CELLS_DEV + obs_offset).astype(jnp.int32)

    def day_info(inputs):
        cell_day, value_day, weight_day = inputs
        basis_rows = basis[cell_day]
        core_day = matmul_high((basis_rows * weight_day[:, None]).T, basis_rows)
        vector_day = matvec_high(basis_rows.T, weight_day * value_day)
        return (core_day, vector_day)
    precision_core, info_vector = lax.map(day_info, (cells, obs_value, obs_weight))

    def filter_step(carry, inputs):
        mean_prev, cov_prev = carry
        decay_day, infl_day, prec_day, vector_day = inputs
        predicted = decay_day[:, None] * cov_prev * decay_day[None, :] + infl_day * prior_cov
        pred_inv = spd_inverse(predicted)
        cov_post = symmetric(spd_inverse(pred_inv + prec_day))
        mean_post = matvec_high(cov_post, matvec_high(pred_inv, decay_day * mean_prev) + vector_day)
        return ((mean_post, cov_post), (mean_post, cov_post))
    start = (jnp.zeros((RANK,), jnp.float32), prior_cov)
    unused, (filt_mean, filtered_covariance) = lax.scan(filter_step, start, (decay, inflation, precision_core, info_vector))

    def smooth_step(carry, inputs):
        mean_next, cov_next = carry
        mean_day, cov_day, decay_next, infl_next = inputs
        predicted = decay_next[:, None] * cov_day * decay_next[None, :] + infl_next * prior_cov
        gain_day = flip_last(spd_solve(predicted, decay_next[:, None] * cov_day))
        mean_smooth = mean_day + matvec_high(gain_day, mean_next - decay_next * mean_day)
        cov_smooth = symmetric(cov_day + matmul_high(matmul_high(gain_day, cov_next - predicted), flip_last(gain_day)))
        return ((mean_smooth, cov_smooth), (mean_smooth, cov_smooth))
    last_state = (filt_mean[-1], filtered_covariance[-1])
    unused_two, (early_mean, early_cov) = lax.scan(smooth_step, last_state, (filt_mean[:-1], filtered_covariance[:-1], decay[1:], inflation[1:]), reverse=True)
    sm_mean = jnp.concatenate([early_mean, filt_mean[-1:]], axis=0)
    sm_cov = jnp.concatenate([early_cov, filtered_covariance[-1:]], axis=0)
    smooth_mean = matmul_high(sm_mean, basis.T)

    def spread_day(cov_day):
        return jnp.sum(matmul_high(basis, cov_day) * basis, axis=1)
    smooth_spread = lax.map(spread_day, sm_cov)
    return (smooth_mean, smooth_spread)
```

```python
import functools

import jax
import jax.numpy as jnp
from jax import lax
from jax.experimental import pallas as pl
from jax.experimental.pallas import tpu as pltpu
from jax.sharding import PartitionSpec as P

HIGHEST = lax.Precision.HIGHEST
MESH = pl.DeviceIdType.MESH
F32 = jnp.float32
BF16 = jnp.bfloat16
LANES = 128
NT = (((1,), (1,)), ((), ()))
NN = (((1,), (0,)), ((), ()))
TN = (((0,), (0,)), ((), ()))


def dot_high(left, right, dims=NN):
    return lax.dot_general(left, right, dims, precision=HIGHEST, preferred_element_type=F32)


def dot_16(left, right, dims=NN):
    return lax.dot_general(left, right, dims, preferred_element_type=F32)


def terms(value, count):
    parts = []
    rest = value
    for step in range(count):
        part = rest.astype(BF16)
        parts.append(part)
        if step < count - 1:
            rest = rest - part.astype(F32)
    return parts


def dot_terms_tn(left, right):
    l1, l2, l3 = terms(left, 3)
    r1, r2, r3 = terms(right, 3)
    return dot_16(
        jnp.concatenate([l1, l1, l2, l2, l1, l3], axis=0),
        jnp.concatenate([r1, r2, r1, r2, r3, r1], axis=0),
        TN,
    )


def bucket_kernel(space_count, cap, owner_ref, offset_ref, value_ref, weight_ref, out_ref):
    days, count = owner_ref.shape
    chunks = count // LANES
    rows_owner = cap // LANES
    slot_rows = space_count * rows_owner
    before = lax.broadcasted_iota(jnp.int32, (LANES, LANES), 0)
    after = lax.broadcasted_iota(jnp.int32, (LANES, LANES), 1)
    earlier = (before < after).astype(F32).astype(BF16)
    ones = jnp.ones((LANES, LANES), BF16)
    owner_row = lax.broadcasted_iota(jnp.int32, (space_count, LANES), 0)
    for day in range(days):
        hits = []
        for chunk in range(chunks):
            own = owner_ref[day : day + 1, chunk * LANES : (chunk + 1) * LANES]
            hits.append((owner_row == own).astype(F32))
        stacked = jnp.concatenate(hits, axis=0).astype(BF16)
        inside = dot_16(stacked, earlier)
        totals = dot_16(stacked, ones)
        base = jnp.zeros((space_count, LANES), F32)
        slots = []
        owner_start = (owner_row * cap).astype(F32)
        for chunk in range(chunks):
            part = slice(chunk * space_count, (chunk + 1) * space_count)
            place = hits[chunk] * (inside[part] + base + owner_start)
            slots.append(jnp.sum(place, axis=0, keepdims=True))
            base = base + totals[part]
        slot = jnp.concatenate(slots, axis=1).astype(jnp.int32)
        slot_high = slot // LANES
        slot_low = slot - slot_high * LANES
        offset = offset_ref[day : day + 1, :]
        offset_high = offset // LANES
        pieces = terms(weight_ref[day : day + 1, :], 3) + terms(value_ref[day : day + 1, :], 3)
        pieces = [piece.astype(F32) for piece in pieces]
        pieces += [offset_high.astype(F32), (offset - offset_high * LANES).astype(F32)]
        in_row = lax.broadcasted_iota(jnp.int32, (slot_rows, count), 0) == slot_high
        left = jnp.concatenate(
            [jnp.where(in_row, piece, 0.0).astype(BF16) for piece in pieces], axis=0
        )
        right = (
            (lax.broadcasted_iota(jnp.int32, (LANES, count), 0) == slot_low)
            .astype(F32)
            .astype(BF16)
        )
        placed = dot_16(left, right, NT)
        cut = [placed[i * slot_rows : (i + 1) * slot_rows] for i in range(8)]
        whole = (cut[0] + cut[1] + cut[2], cut[3] + cut[4] + cut[5], cut[6] * LANES + cut[7])
        for kind in range(3):
            start = (kind * days + day) * rows_owner
            for owner in range(space_count):
                out_ref[owner, start : start + rows_owner, :] = whole[kind][
                    owner * rows_owner : (owner + 1) * rows_owner
                ]


def greet(peers_of, count):
    barrier = pltpu.get_barrier_semaphore()

    def signal(step, _):
        pl.semaphore_signal(barrier, inc=1, device_id=peers_of(step), device_id_type=MESH)
        return _

    lax.fori_loop(1, count, signal, 0)
    pl.semaphore_wait(barrier, count - 1)


def exchange_kernel(space_count, in_ref, out_ref, send_sem, recv_sem, own_sem):
    time_index = lax.axis_index("tm")
    me = lax.axis_index("space")

    def peer(step):
        return lax.rem(me + step, space_count)

    greet(lambda step: (time_index, peer(step)), space_count)

    def copy(step):
        return pltpu.make_async_remote_copy(
            src_ref=in_ref.at[peer(step)],
            dst_ref=out_ref.at[me],
            send_sem=send_sem.at[step],
            recv_sem=recv_sem.at[step],
            device_id=(time_index, peer(step)),
            device_id_type=MESH,
        )

    own = pltpu.make_async_copy(in_ref.at[me], out_ref.at[me], own_sem)
    for step in range(1, space_count):
        copy(step).start()
    own.start()
    own.wait()
    for step in range(1, space_count):
        copy(step).wait()


def sum_kernel(
    time_count, space_count, in_ref, out_ref, held, total, send_sem, recv_sem, send_all, recv_all
):
    time_index = lax.axis_index("tm")
    me = lax.axis_index("space")
    device_count = time_count * space_count

    def peer(step):
        return lax.rem(me + step, space_count)

    def any_peer(step):
        time_peer = lax.rem(time_index + step // space_count, time_count)
        return (time_peer, lax.rem(me + lax.rem(step, space_count), space_count))

    greet(any_peer, device_count)

    def copy(step):
        return pltpu.make_async_remote_copy(
            src_ref=in_ref.at[peer(step)],
            dst_ref=held.at[step],
            send_sem=send_sem.at[step],
            recv_sem=recv_sem.at[step],
            device_id=(time_index, peer(step)),
            device_id_type=MESH,
        )

    for step in range(1, space_count):
        copy(step).start()
    added = in_ref[me]
    for step in range(1, space_count):
        copy(step).wait()
        added = added + held[step]
    total[...] = added
    out_ref[time_index, me] = added

    def share(step):
        return pltpu.make_async_remote_copy(
            src_ref=total,
            dst_ref=out_ref.at[time_index, me],
            send_sem=send_all.at[step],
            recv_sem=recv_all.at[step],
            device_id=any_peer(step),
            device_id_type=MESH,
        )

    def start(step, _):
        share(step).start()
        return _

    def wait(step, _):
        share(step).wait()
        return _

    lax.fori_loop(1, device_count, start, 0)
    lax.fori_loop(1, device_count, wait, 0)


def info_kernel(days, rows_owner, got_ref, back_ref, probe_ref, extra_ref, out_ref, weighted):
    readers = got_ref.shape[0]
    members, cells = back_ref.shape
    rank = probe_ref.shape[0]
    high_count = cells // LANES
    step_rows = 8
    slots = step_rows * LANES
    high_row = lax.broadcasted_iota(jnp.int32, (high_count, slots), 0)
    low_row = lax.broadcasted_iota(jnp.int32, (LANES, slots), 0)
    weight_maps = []
    value_maps = []
    for day in range(days):
        hist = jnp.zeros((4 * high_count, LANES), F32)
        places = [(r, j) for r in range(readers) for j in range(rows_owner)]
        for first in range(0, len(places), step_rows):
            group = places[first : first + step_rows]

            def rows(kind):
                start = (kind * days + day) * rows_owner
                return jnp.concatenate(
                    [got_ref[r, start + j : start + j + 1, :] for r, j in group], axis=1
                )

            weight = rows(0)
            product = weight * rows(1)
            offset = rows(2).astype(jnp.int32)
            high = offset // LANES
            low = offset - high * LANES
            pieces = terms(weight, 2) + terms(product, 2)
            in_row = high_row == high
            left = jnp.concatenate(
                [jnp.where(in_row, piece.astype(F32), 0.0).astype(BF16) for piece in pieces],
                axis=0,
            )
            right = (low_row == low).astype(F32).astype(BF16)
            hist = hist + dot_16(left, right, NT)
        weight_maps.append(hist[:high_count] + hist[high_count : 2 * high_count])
        value_maps.append(hist[2 * high_count : 3 * high_count] + hist[3 * high_count :])

    chunk_rows = 8
    width = chunk_rows * LANES
    vec_row = lax.broadcasted_iota(jnp.int32, (16, width), 0)
    depth = (2 * days + 1) * members + 16
    sums = jnp.zeros((depth, members), F32)
    for first in range(0, high_count, chunk_rows):
        back = back_ref[:, first * LANES : first * LANES + width]
        back_wide = back.astype(F32)
        vectors = jnp.zeros((16, width), F32)
        for day in range(days):
            line = jnp.concatenate(
                [weight_maps[day][j : j + 1] for j in range(first, first + chunk_rows)], axis=1
            )
            part_high, part_low = terms(back_wide * line, 2)
            weighted[2 * day * members : (2 * day + 1) * members, :] = part_high
            weighted[(2 * day + 1) * members : (2 * day + 2) * members, :] = part_low
            line = jnp.concatenate(
                [value_maps[day][j : j + 1] for j in range(first, first + chunk_rows)], axis=1
            )
            line_high, line_low = terms(line, 2)
            vectors = jnp.where(vec_row == day, line_high.astype(F32), vectors)
            vectors = jnp.where(vec_row == day + 8, line_low.astype(F32), vectors)
        weighted[2 * days * members : (2 * days + 1) * members, :] = back
        weighted[(2 * days + 1) * members :, :] = vectors.astype(BF16)
        sums = sums + dot_16(weighted[...], back, NT)

    probe = probe_ref[...]
    columns = []
    for day in range(days):
        info = sums[2 * day * members : (2 * day + 1) * members]
        info = info + sums[(2 * day + 1) * members : (2 * day + 2) * members]
        columns.append(dot_high(dot_high(probe, info), probe, NT))
    gram = sums[2 * days * members : (2 * days + 1) * members]
    tail = sums[(2 * days + 1) * members :]
    vector_rows = tail[:8] + tail[8:]
    side = LANES - days * rank
    vector_rows = jnp.concatenate([vector_rows, jnp.zeros((side - 8, members), F32)], axis=0)
    columns.append(dot_high(probe, vector_rows, NT) + extra_ref[...])
    out_ref[:rank, :] = jnp.concatenate(columns, axis=1)
    out_ref[rank:, :] = jnp.concatenate([gram[:rank], gram[rank:]], axis=1)


def eliminate(mats, rank, only_below):
    row = lax.broadcasted_iota(jnp.int32, (rank, LANES), 0)
    mats = list(mats)
    for k in range(rank):
        for i, mat in enumerate(mats):
            col = mat[:, rank + k : rank + k + 1]
            scaled = mat[k : k + 1, :] * (1.0 / col[k : k + 1, :])
            if only_below:
                mats[i] = mat - jnp.where(row > k, col, 0.0) * scaled
            else:
                mats[i] = jnp.where(row == k, scaled, mat - col * scaled)
    return mats


def factor_rows(mat, rank, eye):
    pivots = jnp.sum(mat[:, rank : 2 * rank] * eye, axis=1, keepdims=True)
    return mat * lax.rsqrt(pivots)


def smooth_kernel(
    days_dev, pay_ref, probe_ref, scale_ref, back_ref, mean_ref, spread_ref, aug_ref, low_ref, top_ref
):
    time_count = pay_ref.shape[0]
    rank, members = probe_ref.shape
    cells = back_ref.shape[1]
    days = time_count * days_dev
    stages = (days - 1).bit_length()
    reach = 1 << (stages - 1)
    rows = lax.broadcasted_iota(jnp.int32, (rank, rank), 0)
    eye = (rows == lax.broadcasted_iota(jnp.int32, (rank, rank), 1)).astype(F32)
    zero = jnp.zeros((rank, rank), F32)
    probe = probe_ref[...]
    gram_pair = pay_ref[0, rank:, :]
    gram = jnp.concatenate([gram_pair[:, :members], gram_pair[:, members:]], axis=0)
    half = dot_high(probe, gram)
    core_gram = dot_high(half, probe, NT)
    reduced = eliminate([jnp.concatenate([zero, core_gram, eye, zero], axis=1)], rank, True)[0]
    lower_inv = factor_rows(reduced, rank, eye)[:, 2 * rank : 3 * rank]
    lower_probe = dot_high(lower_inv, probe)
    projected = dot_high(lower_inv, half)
    scale = scale_ref[...]
    prior = dot_high(projected * (scale * scale), projected, NT)

    def flat(column):
        return jnp.sum(eye * column, axis=0, keepdims=True)

    blocks = [pay_ref[i, :rank, :] for i in range(time_count)]
    side = days_dev * rank
    decay_col = []
    share = []
    for block in blocks:
        for i in range(days_dev):
            decay_col.append(block[:, side + days_dev + i : side + days_dev + i + 1])
            share.append(block[:, side + 2 * days_dev + i : side + 2 * days_dev + i + 1])
    decay_row = [flat(column) for column in decay_col]
    opening = decay_col[0] * prior * decay_row[0] + share[0] * prior
    pair = eliminate(
        [jnp.concatenate([zero, m, eye, zero], axis=1) for m in (prior, opening)], rank, False
    )
    prior_inv = pair[0][:, 2 * rank : 3 * rank]
    opening_inv = pair[1][:, 2 * rank : 3 * rank]
    cores = []
    infos = []
    for block in blocks:
        turned = dot_high(lower_inv, block)
        for i in range(days_dev):
            cores.append(turned[:, i * rank : (i + 1) * rank])
            infos.append(turned[:, side + i : side + i + 1])
    cores = dot_high(jnp.concatenate(cores, axis=0), lower_inv, NT)
    lane = lax.broadcasted_iota(jnp.int32, (rank, rank), 1)
    for t in range(days):
        rate = 1.0 / share[t]
        own = opening_inv if t == 0 else prior_inv * rate
        back = zero if t == 0 else -(prior_inv * decay_row[t]) * rate
        diagonal = own + cores[t * rank : (t + 1) * rank]
        ahead = zero
        if t + 1 < days:
            scaled = decay_col[t + 1] * prior_inv * (1.0 / share[t + 1])
            diagonal = diagonal + scaled * decay_row[t + 1]
            ahead = -scaled
        info = jnp.where(lane == 0, infos[t], 0.0)
        aug_ref[t] = jnp.concatenate([back, diagonal, ahead, info], axis=1)

    blank = jnp.zeros((reach, rank, LANES), F32)
    for ref in (low_ref, top_ref):
        ref[:reach] = blank
        ref[reach + days :] = blank
    wide = lax.broadcasted_iota(jnp.int32, (rank, LANES), 1)
    middle = (wide >= rank) & (wide < 2 * rank)
    last = wide >= 3 * rank

    def stage(index, _):
        distance = jnp.left_shift(1, index)
        mats = [aug_ref[t] for t in range(days)]
        solved = eliminate(mats, rank, False)
        for t in range(days):
            product = dot_terms_tn(aug_ref[t], solved[t])
            top = product[:rank]
            low = product[2 * rank : 3 * rank]
            top_ref[reach + t] = jnp.where(
                middle, pltpu.roll(top, rank, 1), jnp.where(wide >= 2 * rank, top, 0.0)
            )
            low_ref[reach + t] = jnp.where(
                middle,
                pltpu.roll(low, LANES - rank, 1),
                jnp.where((wide < rank) | last, low, 0.0),
            )
        for t in range(days):
            kept = jnp.where(middle | last, aug_ref[t], 0.0)
            aug_ref[t] = kept - low_ref[reach + t - distance] - top_ref[reach + t + distance]
        return _

    lax.fori_loop(0, stages, stage, 0)

    first = lax.axis_index("tm") * days_dev
    own = []
    for i in range(days_dev):
        mat = aug_ref[first + i]
        own.append(jnp.concatenate([eye, mat[:, rank:]], axis=1))
    own = [factor_rows(mat, rank, eye) for mat in eliminate(own, rank, True)]
    roots = jnp.concatenate([mat[:, :rank] for mat in own], axis=0)
    infos = [mat[:, 3 * rank : 3 * rank + 1] for mat in own]
    coefs = terms(dot_high(roots, lower_probe), 3)
    width = 8 * LANES
    for start in range(0, cells, width):
        back = back_ref[:, start : start + width]
        field = dot_16(coefs[0], back) + dot_16(coefs[1], back) + dot_16(coefs[2], back)
        for i in range(days_dev):
            part = field[i * rank : (i + 1) * rank]
            mean_ref[i : i + 1, start : start + width] = jnp.sum(
                part * infos[i], axis=0, keepdims=True
            )
            spread_ref[i : i + 1, start : start + width] = jnp.sum(
                part * part, axis=0, keepdims=True
            )


VMEM = pl.BlockSpec(memory_space=pltpu.VMEM)
PARAMS = pltpu.CompilerParams(vmem_limit_bytes=48 * 1024 * 1024)


def body(
    background, probe, member_scale, decay, inflation, obs_owner, obs_offset, obs_value, obs_weight
):
    members, rank = probe.shape
    cells = background.shape[0]
    days_dev = decay.shape[0]
    obs_dev = obs_offset.shape[1]
    space_count = lax.axis_size("space")
    time_count = lax.axis_size("tm")
    days = days_dev * time_count
    cap = 2 * obs_dev // space_count
    rows_owner = cap // LANES
    scaled = (probe.astype(F32) * member_scale[:, None]).astype(BF16)
    probe_rows = scaled.astype(F32).T
    back = background.T
    first_space = lax.axis_index("space") == 0
    extra = jnp.concatenate(
        [
            jnp.zeros((rank, days_dev), F32),
            decay.T,
            jnp.broadcast_to(inflation[None, :], (rank, days_dev)),
            jnp.zeros((rank, LANES - days_dev * rank - 3 * days_dev), F32),
        ],
        axis=1,
    )
    extra = jnp.where(first_space, extra, 0.0)

    slab = (space_count, 3 * days_dev * rows_owner, LANES)
    buckets = pl.pallas_call(
        functools.partial(bucket_kernel, space_count, cap),
        out_shape=jax.ShapeDtypeStruct(slab, F32),
        in_specs=[VMEM] * 4,
        out_specs=VMEM,
        compiler_params=PARAMS,
        name="buckets",
    )(obs_owner[:, :, 0], obs_offset, obs_value, obs_weight)
    received = pl.pallas_call(
        functools.partial(exchange_kernel, space_count),
        out_shape=jax.ShapeDtypeStruct(slab, F32),
        in_specs=[VMEM],
        out_specs=VMEM,
        scratch_shapes=[
            pltpu.SemaphoreType.DMA((space_count,)),
            pltpu.SemaphoreType.DMA((space_count,)),
            pltpu.SemaphoreType.DMA,
        ],
        compiler_params=pltpu.CompilerParams(
            collective_id=0, has_side_effects=True, vmem_limit_bytes=48 * 1024 * 1024
        ),
        name="exchange",
    )(buckets)
    payload = pl.pallas_call(
        functools.partial(info_kernel, days_dev, rows_owner),
        out_shape=jax.ShapeDtypeStruct((rank + members // 2, LANES), F32),
        in_specs=[VMEM] * 4,
        out_specs=VMEM,
        scratch_shapes=[pltpu.VMEM(((2 * days_dev + 1) * members + 16, 8 * LANES), BF16)],
        compiler_params=PARAMS,
        name="information",
    )(received, back, probe_rows, extra)
    height = payload.shape[0] // space_count
    summed = pl.pallas_call(
        functools.partial(sum_kernel, time_count, space_count),
        out_shape=jax.ShapeDtypeStruct((time_count, space_count, height, LANES), F32),
        in_specs=[VMEM],
        out_specs=VMEM,
        scratch_shapes=[
            pltpu.VMEM((space_count, height, LANES), F32),
            pltpu.VMEM((height, LANES), F32),
            pltpu.SemaphoreType.DMA((space_count,)),
            pltpu.SemaphoreType.DMA((space_count,)),
            pltpu.SemaphoreType.DMA((time_count * space_count,)),
            pltpu.SemaphoreType.DMA((time_count * space_count,)),
        ],
        compiler_params=pltpu.CompilerParams(
            collective_id=1, has_side_effects=True, vmem_limit_bytes=48 * 1024 * 1024
        ),
        name="sums",
    )(payload.reshape(space_count, height, LANES))
    reach = 1 << ((days - 1).bit_length() - 1)
    return pl.pallas_call(
        functools.partial(smooth_kernel, days_dev),
        out_shape=[jax.ShapeDtypeStruct((days_dev, cells), F32)] * 2,
        in_specs=[VMEM] * 4,
        out_specs=[VMEM] * 2,
        scratch_shapes=[
            pltpu.VMEM((days, rank, LANES), F32),
            pltpu.VMEM((days + 2 * reach, rank, LANES), F32),
            pltpu.VMEM((days + 2 * reach, rank, LANES), F32),
        ],
        compiler_params=PARAMS,
        name="smoother",
    )(summed.reshape(time_count, payload.shape[0], LANES), probe_rows, member_scale[None, :], back)


def solution(mesh):
    return jax.shard_map(
        body,
        mesh=mesh,
        in_specs=(
            P("space", None),
            P(),
            P(),
            P("tm", None),
            P("tm"),
            P("tm", "space", None),
            P("tm", "space"),
            P("tm", "space"),
            P("tm", "space"),
        ),
        out_specs=(P("tm", "space"), P("tm", "space")),
        check_vma=False,
    )
```

```python
import functools

import jax
import jax.numpy as jnp
from jax import lax
from jax.experimental import pallas as pl
from jax.experimental.pallas import tpu as pltpu
from jax.sharding import PartitionSpec as P

HIGHEST = lax.Precision.HIGHEST
MESH = pl.DeviceIdType.MESH
F32 = jnp.float32
BF16 = jnp.bfloat16
LANES = 128
NT = (((1,), (1,)), ((), ()))
NN = (((1,), (0,)), ((), ()))
TN = (((0,), (0,)), ((), ()))


def dot_high(left, right, dims=NN):
    return lax.dot_general(left, right, dims, precision=HIGHEST, preferred_element_type=F32)


def dot_16(left, right, dims=NN):
    return lax.dot_general(left, right, dims, preferred_element_type=F32)


def terms(value, count):
    parts = []
    rest = value
    for step in range(count):
        part = rest.astype(BF16)
        parts.append(part)
        if step < count - 1:
            rest = rest - part.astype(F32)
    return parts


def dot_terms_tn(left, right):
    l1, l2, l3 = terms(left, 3)
    r1, r2, r3 = terms(right, 3)
    return dot_16(
        jnp.concatenate([l1, l1, l2, l2, l1, l3], axis=0),
        jnp.concatenate([r1, r2, r1, r2, r3, r1], axis=0),
        TN,
    )


def make_buckets(space_count, cap, owner_ref, offset_ref, value_ref, weight_ref, out_ref):
    days, count = offset_ref.shape
    chunks = count // LANES
    rows_owner = cap // LANES
    slot_rows = space_count * rows_owner
    before = lax.broadcasted_iota(jnp.int32, (LANES, LANES), 0)
    after = lax.broadcasted_iota(jnp.int32, (LANES, LANES), 1)
    earlier = (before < after).astype(F32).astype(BF16)
    ones = jnp.ones((LANES, LANES), BF16)
    owner_row = lax.broadcasted_iota(jnp.int32, (space_count, LANES), 0)
    for day in range(days):
        hits = []
        for chunk in range(chunks):
            own = owner_ref[day, :, chunk * LANES : (chunk + 1) * LANES]
            hits.append((owner_row == own).astype(F32))
        stacked = jnp.concatenate(hits, axis=0).astype(BF16)
        inside = dot_16(stacked, earlier)
        totals = dot_16(stacked, ones)
        base = (owner_row * cap).astype(F32)
        slots = []
        for chunk in range(chunks):
            part = slice(chunk * space_count, (chunk + 1) * space_count)
            place = hits[chunk] * (inside[part] + base)
            slots.append(jnp.sum(place, axis=0, keepdims=True))
            base = base + totals[part]
        slot = jnp.concatenate(slots, axis=1).astype(jnp.int32)
        slot_high = slot // LANES
        slot_low = slot - slot_high * LANES
        offset = offset_ref[day : day + 1, :]
        offset_high = offset // LANES
        pieces = terms(weight_ref[day : day + 1, :], 3) + terms(value_ref[day : day + 1, :], 3)
        pieces = [piece.astype(F32) for piece in pieces]
        pieces += [offset_high.astype(F32), (offset - offset_high * LANES).astype(F32)]
        in_row = lax.broadcasted_iota(jnp.int32, (slot_rows, count), 0) == slot_high
        left = jnp.concatenate(
            [jnp.where(in_row, piece, 0.0).astype(BF16) for piece in pieces], axis=0
        )
        right = (
            (lax.broadcasted_iota(jnp.int32, (LANES, count), 0) == slot_low)
            .astype(F32)
            .astype(BF16)
        )
        placed = dot_16(left, right, NT)
        cut = [placed[i * slot_rows : (i + 1) * slot_rows] for i in range(8)]
        whole = (cut[0] + cut[1] + cut[2], cut[3] + cut[4] + cut[5], cut[6] * LANES + cut[7])
        for kind in range(3):
            start = (kind * days + day) * rows_owner
            for owner in range(space_count):
                out_ref[owner, start : start + rows_owner, :] = whole[kind][
                    owner * rows_owner : (owner + 1) * rows_owner
                ]


def gather_kernel(
    time_count,
    space_count,
    cap,
    owner_hbm,
    offset_hbm,
    value_hbm,
    weight_hbm,
    back_hbm,
    probe_ref,
    extra_ref,
    out_ref,
    owner_ref,
    offset_ref,
    value_ref,
    weight_ref,
    back_ref,
    sent,
    got,
    weighted,
    hists,
    payload,
    held,
    local_sem,
    send_sem,
    recv_sem,
    send_sum,
    recv_sum,
    send_time,
    recv_time,
    send_all,
    recv_all,
):
    time_index = lax.axis_index("tm")
    me = lax.axis_index("space")
    days = offset_ref.shape[0]
    rows_owner = cap // LANES
    members, cells = back_ref.shape
    rank = probe_ref.shape[0]
    high_count = cells // LANES

    def space_peer(step):
        return (time_index, lax.rem(me + step, space_count))

    def time_peer(step):
        return (lax.rem(time_index + step, time_count), me)

    loads = [
        pltpu.make_async_copy(source, target, local_sem.at[i])
        for i, (source, target) in enumerate(
            (
                (owner_hbm, owner_ref),
                (offset_hbm, offset_ref),
                (value_hbm, value_ref),
                (weight_hbm, weight_ref),
                (back_hbm, back_ref),
            )
        )
    ]
    for load in loads:
        load.start()
    barrier = pltpu.get_barrier_semaphore()
    for step in range(1, space_count):
        pl.semaphore_signal(barrier, inc=1, device_id=space_peer(step), device_id_type=MESH)
    for step in range(1, time_count):
        pl.semaphore_signal(barrier, inc=1, device_id=time_peer(step), device_id_type=MESH)
    for load in loads[:4]:
        load.wait()
    make_buckets(space_count, cap, owner_ref, offset_ref, value_ref, weight_ref, sent)
    pl.semaphore_wait(barrier, space_count + time_count - 2)

    def space_copy(step, source, target, sends, receives):
        return pltpu.make_async_remote_copy(
            src_ref=source,
            dst_ref=target,
            send_sem=sends.at[step],
            recv_sem=receives.at[step],
            device_id=space_peer(step),
            device_id_type=MESH,
        )

    copies = [
        space_copy(step, sent.at[space_peer(step)[1]], got.at[step], send_sem, recv_sem)
        for step in range(1, space_count)
    ]
    for copy in copies:
        copy.start()
    loads[4].wait()

    slots = rows_owner * LANES
    high_row = lax.broadcasted_iota(jnp.int32, (high_count, slots), 0)
    low_row = lax.broadcasted_iota(jnp.int32, (LANES, slots), 0)
    for step in range(space_count):
        if step > 0:
            copies[step - 1].wait()
            slab = got[step]
        else:
            slab = sent[me]
        for day in range(days):

            def rows(kind):
                start = (kind * days + day) * rows_owner
                return jnp.concatenate(
                    [slab[start + j : start + j + 1, :] for j in range(rows_owner)], axis=1
                )

            weight = rows(0)
            product = weight * rows(1)
            offset = rows(2).astype(jnp.int32)
            high = offset // LANES
            low = offset - high * LANES
            pieces = terms(weight, 2) + terms(product, 2)
            in_row = high_row == high
            left = jnp.concatenate(
                [jnp.where(in_row, piece.astype(F32), 0.0).astype(BF16) for piece in pieces],
                axis=0,
            )
            right = (low_row == low).astype(F32).astype(BF16)
            part = dot_16(left, right, NT)
            hists[day] = part if step == 0 else hists[day] + part
    weight_maps = []
    value_maps = []
    for day in range(days):
        hist = hists[day]
        weight_maps.append(hist[:high_count] + hist[high_count : 2 * high_count])
        value_maps.append(hist[2 * high_count : 3 * high_count] + hist[3 * high_count :])

    chunk_rows = 8
    width = chunk_rows * LANES
    vec_row = lax.broadcasted_iota(jnp.int32, (16, width), 0)
    depth = (2 * days + 1) * members + 16
    sums = jnp.zeros((depth, members), F32)
    for first in range(0, high_count, chunk_rows):
        back = back_ref[:, first * LANES : first * LANES + width]
        back_wide = back.astype(F32)
        vectors = jnp.zeros((16, width), F32)
        for day in range(days):
            line = jnp.concatenate(
                [weight_maps[day][j : j + 1] for j in range(first, first + chunk_rows)], axis=1
            )
            part_high, part_low = terms(back_wide * line, 2)
            weighted[2 * day * members : (2 * day + 1) * members, :] = part_high
            weighted[(2 * day + 1) * members : (2 * day + 2) * members, :] = part_low
            line = jnp.concatenate(
                [value_maps[day][j : j + 1] for j in range(first, first + chunk_rows)], axis=1
            )
            line_high, line_low = terms(line, 2)
            vectors = jnp.where(vec_row == day, line_high.astype(F32), vectors)
            vectors = jnp.where(vec_row == day + 8, line_low.astype(F32), vectors)
        weighted[2 * days * members : (2 * days + 1) * members, :] = back
        weighted[(2 * days + 1) * members :, :] = vectors.astype(BF16)
        sums = sums + dot_16(weighted[...], back, NT)

    probe = probe_ref[...]
    infos = [
        sums[2 * day * members : (2 * day + 1) * members]
        + sums[(2 * day + 1) * members : (2 * day + 2) * members]
        for day in range(days)
    ]
    turned = dot_high(jnp.concatenate(infos, axis=0), probe, NT)
    columns = [
        dot_high(probe, turned[day * members : (day + 1) * members]) for day in range(days)
    ]
    gram = sums[2 * days * members : (2 * days + 1) * members]
    tail = sums[(2 * days + 1) * members :]
    vector_rows = tail[:8] + tail[8:]
    side = LANES - days * rank
    vector_rows = jnp.concatenate([vector_rows, jnp.zeros((side - 8, members), F32)], axis=0)
    columns.append(dot_high(probe, vector_rows, NT) + extra_ref[...])
    upper = jnp.concatenate(columns, axis=1)
    lower = jnp.concatenate([gram[:rank], gram[rank:]], axis=1)
    height = payload.shape[1]
    for i in range(space_count):
        start = i * height
        payload[i] = (
            upper[start : start + height] if start < rank else lower[start - rank : start - rank + height]
        )

    copies = [
        space_copy(step, payload.at[space_peer(step)[1]], held.at[step], send_sum, recv_sum)
        for step in range(1, space_count)
    ]
    for copy in copies:
        copy.start()
    added = payload[me]
    for step in range(1, space_count):
        copies[step - 1].wait()
        added = added + held[step]
    out_ref[me, time_index] = added
    copies = [
        pltpu.make_async_remote_copy(
            src_ref=out_ref.at[me, time_index],
            dst_ref=out_ref.at[me, time_index],
            send_sem=send_time.at[step],
            recv_sem=recv_time.at[step],
            device_id=time_peer(step),
            device_id_type=MESH,
        )
        for step in range(1, time_count)
    ]
    for copy in copies:
        copy.start()
    for copy in copies:
        copy.wait()
    copies = [
        space_copy(step, out_ref.at[me], out_ref.at[me], send_all, recv_all)
        for step in range(1, space_count)
    ]
    for copy in copies:
        copy.start()
    for copy in copies:
        copy.wait()


def eliminate(mats, rank, only_below):
    row = lax.broadcasted_iota(jnp.int32, (rank, LANES), 0)
    mats = list(mats)
    for k in range(0, rank, 2):
        for i, mat in enumerate(mats):
            col_a = mat[:, rank + k : rank + k + 1]
            col_b = mat[:, rank + k + 1 : rank + k + 2]
            a, b = col_a[k : k + 1, :], col_b[k : k + 1, :]
            c = col_b[k + 1 : k + 2, :]
            row_a, row_b = mat[k : k + 1, :], mat[k + 1 : k + 2, :]
            scale = 1.0 / (a * c - b * b)
            new_a = (c * row_a - b * row_b) * scale
            new_b = (a * row_b - b * row_a) * scale
            update = mat - col_a * new_a - col_b * new_b
            if only_below:
                second = row_b - (b / a) * row_a
                mats[i] = jnp.where(
                    row > k + 1, update, jnp.where(row == k + 1, second, mat)
                )
            else:
                mats[i] = jnp.where(row == k, new_a, jnp.where(row == k + 1, new_b, update))
    return mats


def factor_rows(mat, rank, eye):
    pivots = jnp.sum(mat[:, rank : 2 * rank] * eye, axis=1, keepdims=True)
    return mat * lax.rsqrt(pivots)


def smooth_kernel(
    days_dev,
    pay_ref,
    probe_ref,
    scale_ref,
    back_hbm,
    mean_ref,
    spread_ref,
    aug_ref,
    low_ref,
    top_ref,
    back_ref,
    back_sem,
):
    load = pltpu.make_async_copy(back_hbm, back_ref, back_sem)
    load.start()
    space_count, time_count, height = pay_ref.shape[:3]
    rank, members = probe_ref.shape
    cells = back_ref.shape[1]
    days = time_count * days_dev
    stages = (days - 1).bit_length()
    reach = 1 << (stages - 1)
    rows = lax.broadcasted_iota(jnp.int32, (rank, rank), 0)
    eye = (rows == lax.broadcasted_iota(jnp.int32, (rank, rank), 1)).astype(F32)
    zero = jnp.zeros((rank, rank), F32)
    probe = probe_ref[...]
    upper_count = rank // height
    gram_pair = jnp.concatenate(
        [pay_ref[s, 0] for s in range(upper_count, space_count)], axis=0
    )
    gram = jnp.concatenate([gram_pair[:, :members], gram_pair[:, members:]], axis=0)
    half = dot_high(probe, gram)
    core_gram = dot_high(half, probe, NT)
    reduced = eliminate([jnp.concatenate([zero, core_gram, eye, zero], axis=1)], rank, True)[0]
    lower_inv = factor_rows(reduced, rank, eye)[:, 2 * rank : 3 * rank]
    lower_probe = dot_high(lower_inv, probe)
    projected = dot_high(lower_inv, half)
    scale = scale_ref[...]
    prior = dot_high(projected * (scale * scale), projected, NT)

    def flat(column):
        return jnp.sum(eye * column, axis=0, keepdims=True)

    blocks = [
        jnp.concatenate([pay_ref[s, i] for s in range(upper_count)], axis=0)
        for i in range(time_count)
    ]
    side = days_dev * rank
    decay_col = []
    share = []
    for block in blocks:
        for i in range(days_dev):
            decay_col.append(block[:, side + days_dev + i : side + days_dev + i + 1])
            share.append(block[:, side + 2 * days_dev + i : side + 2 * days_dev + i + 1])
    decay_row = [flat(column) for column in decay_col]
    opening = decay_col[0] * prior * decay_row[0] + share[0] * prior
    pair = eliminate(
        [jnp.concatenate([zero, m, eye, zero], axis=1) for m in (prior, opening)], rank, False
    )
    prior_inv = pair[0][:, 2 * rank : 3 * rank]
    opening_inv = pair[1][:, 2 * rank : 3 * rank]
    cores = []
    infos = []
    for block in blocks:
        turned = dot_high(lower_inv, block)
        for i in range(days_dev):
            cores.append(turned[:, i * rank : (i + 1) * rank])
            infos.append(turned[:, side + i : side + i + 1])
    cores = dot_high(jnp.concatenate(cores, axis=0), lower_inv, NT)
    lane = lax.broadcasted_iota(jnp.int32, (rank, rank), 1)
    for t in range(days):
        rate = 1.0 / share[t]
        own = opening_inv if t == 0 else prior_inv * rate
        back = zero if t == 0 else -(prior_inv * decay_row[t]) * rate
        diagonal = own + cores[t * rank : (t + 1) * rank]
        ahead = zero
        if t + 1 < days:
            scaled = decay_col[t + 1] * prior_inv * (1.0 / share[t + 1])
            diagonal = diagonal + scaled * decay_row[t + 1]
            ahead = -scaled
        info = jnp.where(lane == 0, infos[t], 0.0)
        aug_ref[t] = jnp.concatenate([back, diagonal, ahead, info], axis=1)

    blank = jnp.zeros((reach, rank, LANES), F32)
    for ref in (low_ref, top_ref):
        ref[:reach] = blank
        ref[reach + days :] = blank
    wide = lax.broadcasted_iota(jnp.int32, (rank, LANES), 1)
    middle = (wide >= rank) & (wide < 2 * rank)
    last = wide >= 3 * rank

    def stage(index, _):
        distance = jnp.left_shift(1, index)
        mats = [aug_ref[t] for t in range(days)]
        solved = eliminate(mats, rank, False)
        for t in range(days):
            product = dot_terms_tn(aug_ref[t], solved[t])
            top = product[:rank]
            low = product[2 * rank : 3 * rank]
            top_ref[reach + t] = jnp.where(
                middle, pltpu.roll(top, rank, 1), jnp.where(wide >= 2 * rank, top, 0.0)
            )
            low_ref[reach + t] = jnp.where(
                middle,
                pltpu.roll(low, LANES - rank, 1),
                jnp.where((wide < rank) | last, low, 0.0),
            )
        for t in range(days):
            kept = jnp.where(middle | last, aug_ref[t], 0.0)
            aug_ref[t] = kept - low_ref[reach + t - distance] - top_ref[reach + t + distance]
        return _

    lax.fori_loop(0, stages, stage, 0)

    first = lax.axis_index("tm") * days_dev
    own = []
    for i in range(days_dev):
        mat = aug_ref[first + i]
        own.append(jnp.concatenate([eye, mat[:, rank:]], axis=1))
    own = [factor_rows(mat, rank, eye) for mat in eliminate(own, rank, True)]
    roots = jnp.concatenate([mat[:, :rank] for mat in own], axis=0)
    infos = [mat[:, 3 * rank : 3 * rank + 1] for mat in own]
    coefs = terms(dot_high(roots, lower_probe), 3)
    width = 8 * LANES
    load.wait()
    for start in range(0, cells, width):
        back = back_ref[:, start : start + width]
        field = dot_16(coefs[0], back) + dot_16(coefs[1], back) + dot_16(coefs[2], back)
        for i in range(days_dev):
            part = field[i * rank : (i + 1) * rank]
            mean_ref[i : i + 1, start : start + width] = jnp.sum(
                part * infos[i], axis=0, keepdims=True
            )
            spread_ref[i : i + 1, start : start + width] = jnp.sum(
                part * part, axis=0, keepdims=True
            )


VMEM = pl.BlockSpec(memory_space=pltpu.VMEM)
ANY = pl.BlockSpec(memory_space=pl.ANY)
PARAMS = pltpu.CompilerParams(vmem_limit_bytes=56 * 1024 * 1024)


def body(
    background, probe, member_scale, decay, inflation, obs_owner, obs_offset, obs_value, obs_weight
):
    members, rank = probe.shape
    cells = background.shape[0]
    days_dev = decay.shape[0]
    obs_dev = obs_offset.shape[1]
    space_count = lax.axis_size("space")
    time_count = lax.axis_size("tm")
    days = days_dev * time_count
    cap = 2 * obs_dev // space_count
    rows_owner = cap // LANES
    scaled = (probe.astype(F32) * member_scale[:, None]).astype(BF16)
    probe_rows = scaled.astype(F32).T
    back = background.T
    first_space = lax.axis_index("space") == 0
    extra = jnp.concatenate(
        [
            jnp.zeros((rank, days_dev), F32),
            decay.T,
            jnp.broadcast_to(inflation[None, :], (rank, days_dev)),
            jnp.zeros((rank, LANES - days_dev * rank - 3 * days_dev), F32),
        ],
        axis=1,
    )
    extra = jnp.where(first_space, extra, 0.0)

    slab = (space_count, 3 * days_dev * rows_owner, LANES)
    height = (rank + members // 2) // space_count
    part = (space_count, height, LANES)
    dma = pltpu.SemaphoreType.DMA
    summed = pl.pallas_call(
        functools.partial(gather_kernel, time_count, space_count, cap),
        out_shape=jax.ShapeDtypeStruct((space_count, time_count, height, LANES), F32),
        in_specs=[ANY] * 5 + [VMEM] * 2,
        out_specs=VMEM,
        scratch_shapes=[
            pltpu.VMEM((days_dev, 1, obs_dev), jnp.int32),
            pltpu.VMEM((days_dev, obs_dev), jnp.int32),
            pltpu.VMEM((days_dev, obs_dev), F32),
            pltpu.VMEM((days_dev, obs_dev), F32),
            pltpu.VMEM((members, cells), BF16),
            pltpu.VMEM(slab, F32),
            pltpu.VMEM(slab, F32),
            pltpu.VMEM(((2 * days_dev + 1) * members + 16, 8 * LANES), BF16),
            pltpu.VMEM((days_dev, 4 * (cells // LANES), LANES), F32),
            pltpu.VMEM(part, F32),
            pltpu.VMEM(part, F32),
            dma((5,)),
            dma((space_count,)),
            dma((space_count,)),
            dma((space_count,)),
            dma((space_count,)),
            dma((time_count,)),
            dma((time_count,)),
            dma((space_count,)),
            dma((space_count,)),
        ],
        compiler_params=pltpu.CompilerParams(
            collective_id=0, has_side_effects=True, vmem_limit_bytes=56 * 1024 * 1024
        ),
        name="gather",
    )(
        jnp.swapaxes(obs_owner, 1, 2),
        obs_offset,
        obs_value,
        obs_weight,
        back,
        probe_rows,
        extra,
    )
    reach = 1 << ((days - 1).bit_length() - 1)
    return pl.pallas_call(
        functools.partial(smooth_kernel, days_dev),
        out_shape=[jax.ShapeDtypeStruct((days_dev, cells), F32)] * 2,
        in_specs=[VMEM] * 3 + [ANY],
        out_specs=[VMEM] * 2,
        scratch_shapes=[
            pltpu.VMEM((days, rank, LANES), F32),
            pltpu.VMEM((days + 2 * reach, rank, LANES), F32),
            pltpu.VMEM((days + 2 * reach, rank, LANES), F32),
            pltpu.VMEM((members, cells), BF16),
            pltpu.SemaphoreType.DMA,
        ],
        compiler_params=PARAMS,
        name="smoother",
    )(summed, probe_rows, member_scale[None, :], back)


def solution(mesh):
    return jax.shard_map(
        body,
        mesh=mesh,
        in_specs=(
            P("space", None),
            P(),
            P(),
            P("tm", None),
            P("tm"),
            P("tm", "space", None),
            P("tm", "space"),
            P("tm", "space"),
            P("tm", "space"),
        ),
        out_specs=(P("tm", "space"), P("tm", "space")),
        check_vma=False,
    )
```

```python
import functools

import jax
import jax.numpy as jnp
from jax import lax
from jax.experimental import pallas as pl
from jax.experimental.pallas import tpu as pltpu
from jax.sharding import PartitionSpec as P

HIGHEST = lax.Precision.HIGHEST
MESH = pl.DeviceIdType.MESH
F32 = jnp.float32
BF16 = jnp.bfloat16
LANES = 128
NT = (((1,), (1,)), ((), ()))
NN = (((1,), (0,)), ((), ()))
TN = (((0,), (0,)), ((), ()))


def dot_high(left, right, dims=NN):
    return lax.dot_general(left, right, dims, precision=HIGHEST, preferred_element_type=F32)


def dot_16(left, right, dims=NN):
    return lax.dot_general(left, right, dims, preferred_element_type=F32)


def terms(value, count):
    parts = []
    rest = value
    for step in range(count):
        part = rest.astype(BF16)
        parts.append(part)
        if step < count - 1:
            rest = rest - part.astype(F32)
    return parts


def dot_terms_tn(left, right):
    l1, l2, l3 = terms(left, 3)
    r1, r2, r3 = terms(right, 3)
    return dot_16(
        jnp.concatenate([l1, l1, l2, l2, l1, l3], axis=0),
        jnp.concatenate([r1, r2, r1, r2, r3, r1], axis=0),
        TN,
    )


def scaled_rows(probe_ref, scale_ref):
    scaled = (probe_ref[...].astype(F32) * scale_ref[...]).astype(BF16)
    return scaled.astype(F32)


def make_buckets(space_count, cap, owner_ref, offset_ref, value_ref, weight_ref, out_ref):
    days, count = offset_ref.shape
    chunks = count // LANES
    rows_owner = cap // LANES
    slot_rows = space_count * rows_owner
    before = lax.broadcasted_iota(jnp.int32, (LANES, LANES), 0)
    after = lax.broadcasted_iota(jnp.int32, (LANES, LANES), 1)
    earlier = (before < after).astype(F32).astype(BF16)
    ones = jnp.ones((LANES, LANES), BF16)
    owner_row = lax.broadcasted_iota(jnp.int32, (space_count, LANES), 0)
    for day in range(days):
        hits = []
        for chunk in range(chunks):
            own = owner_ref[day, :, chunk * LANES : (chunk + 1) * LANES]
            hits.append((owner_row == own).astype(F32))
        stacked = jnp.concatenate(hits, axis=0).astype(BF16)
        inside = dot_16(stacked, earlier)
        totals = dot_16(stacked, ones)
        base = (owner_row * cap).astype(F32)
        slots = []
        for chunk in range(chunks):
            part = slice(chunk * space_count, (chunk + 1) * space_count)
            place = hits[chunk] * (inside[part] + base)
            slots.append(jnp.sum(place, axis=0, keepdims=True))
            base = base + totals[part]
        slot = jnp.concatenate(slots, axis=1).astype(jnp.int32)
        slot_high = slot // LANES
        slot_low = slot - slot_high * LANES
        offset = offset_ref[day : day + 1, :]
        offset_high = offset // LANES
        pieces = terms(weight_ref[day : day + 1, :], 3) + terms(value_ref[day : day + 1, :], 3)
        pieces = [piece.astype(F32) for piece in pieces]
        pieces += [offset_high.astype(F32), (offset - offset_high * LANES).astype(F32)]
        in_row = lax.broadcasted_iota(jnp.int32, (slot_rows, count), 0) == slot_high
        left = jnp.concatenate(
            [jnp.where(in_row, piece, 0.0).astype(BF16) for piece in pieces], axis=0
        )
        right = (
            (lax.broadcasted_iota(jnp.int32, (LANES, count), 0) == slot_low)
            .astype(F32)
            .astype(BF16)
        )
        placed = dot_16(left, right, NT)
        cut = [placed[i * slot_rows : (i + 1) * slot_rows] for i in range(8)]
        whole = (cut[0] + cut[1] + cut[2], cut[3] + cut[4] + cut[5], cut[6] * LANES + cut[7])
        for kind in range(3):
            start = (kind * days + day) * rows_owner
            for owner in range(space_count):
                out_ref[owner, start : start + rows_owner, :] = whole[kind][
                    owner * rows_owner : (owner + 1) * rows_owner
                ]


def gather_kernel(
    time_count,
    space_count,
    cap,
    owner_hbm,
    offset_hbm,
    value_hbm,
    weight_hbm,
    back_hbm,
    probe_hbm,
    scale_hbm,
    decay_hbm,
    inflation_hbm,
    out_ref,
    owner_ref,
    offset_ref,
    value_ref,
    weight_ref,
    back_ref,
    probe_ref,
    scale_ref,
    decay_ref,
    inflation_ref,
    sent,
    got,
    weighted,
    hists,
    payload,
    held,
    local_sem,
    send_sem,
    recv_sem,
    send_sum,
    recv_sum,
    send_time,
    recv_time,
    send_all,
    recv_all,
):
    time_index = lax.axis_index("tm")
    me = lax.axis_index("space")
    days = offset_ref.shape[0]
    rows_owner = cap // LANES
    members, cells = back_ref.shape
    rank = probe_ref.shape[0]
    high_count = cells // LANES

    def space_peer(step):
        return (time_index, lax.rem(me + step, space_count))

    def time_peer(step):
        return (lax.rem(time_index + step, time_count), me)

    loads = [
        pltpu.make_async_copy(source, target, local_sem.at[i])
        for i, (source, target) in enumerate(
            (
                (owner_hbm, owner_ref),
                (offset_hbm, offset_ref),
                (value_hbm, value_ref),
                (weight_hbm, weight_ref),
                (back_hbm, back_ref),
                (probe_hbm, probe_ref),
                (scale_hbm, scale_ref),
                (decay_hbm, decay_ref),
                (inflation_hbm, inflation_ref),
            )
        )
    ]
    for load in loads:
        load.start()
    barrier = pltpu.get_barrier_semaphore()
    for step in range(1, space_count):
        pl.semaphore_signal(barrier, inc=1, device_id=space_peer(step), device_id_type=MESH)
    for step in range(1, time_count):
        pl.semaphore_signal(barrier, inc=1, device_id=time_peer(step), device_id_type=MESH)
    for load in loads[:4]:
        load.wait()
    make_buckets(space_count, cap, owner_ref, offset_ref, value_ref, weight_ref, sent)
    pl.semaphore_wait(barrier, space_count + time_count - 2)

    def space_copy(step, source, target, sends, receives):
        return pltpu.make_async_remote_copy(
            src_ref=source,
            dst_ref=target,
            send_sem=sends.at[step],
            recv_sem=receives.at[step],
            device_id=space_peer(step),
            device_id_type=MESH,
        )

    copies = [
        space_copy(step, sent.at[space_peer(step)[1]], got.at[step], send_sem, recv_sem)
        for step in range(1, space_count)
    ]
    for copy in copies:
        copy.start()
    for load in loads[4:]:
        load.wait()
    probe = scaled_rows(probe_ref, scale_ref)
    at_row = lax.broadcasted_iota(jnp.int32, (rank, rank), 0)
    at_lane = lax.broadcasted_iota(jnp.int32, (rank, rank), 1)
    side = LANES - days * rank
    side_lane = lax.broadcasted_iota(jnp.int32, (rank, side), 1)
    extra = jnp.zeros((rank, side), F32)
    for day in range(days):
        line = jnp.where(at_row == at_lane, decay_ref[day : day + 1, :], 0.0)
        column = jnp.sum(line, axis=1, keepdims=True)
        extra = jnp.where(side_lane == days + day, column, extra)
        share = inflation_ref[:, day : day + 1]
        extra = jnp.where(side_lane == 2 * days + day, share, extra)
    extra = extra * (me == 0).astype(F32)

    slots = rows_owner * LANES
    high_row = lax.broadcasted_iota(jnp.int32, (high_count, slots), 0)
    low_row = lax.broadcasted_iota(jnp.int32, (LANES, slots), 0)
    for step in range(space_count):
        if step > 0:
            copies[step - 1].wait()
            slab = got[step]
        else:
            slab = sent[me]
        for day in range(days):

            def rows(kind):
                start = (kind * days + day) * rows_owner
                return jnp.concatenate(
                    [slab[start + j : start + j + 1, :] for j in range(rows_owner)], axis=1
                )

            weight = rows(0)
            product = weight * rows(1)
            offset = rows(2).astype(jnp.int32)
            high = offset // LANES
            low = offset - high * LANES
            pieces = terms(weight, 2) + terms(product, 2)
            in_row = high_row == high
            left = jnp.concatenate(
                [jnp.where(in_row, piece.astype(F32), 0.0).astype(BF16) for piece in pieces],
                axis=0,
            )
            right = (low_row == low).astype(F32).astype(BF16)
            part = dot_16(left, right, NT)
            hists[day] = part if step == 0 else hists[day] + part
    weight_maps = []
    value_maps = []
    for day in range(days):
        hist = hists[day]
        weight_maps.append(hist[:high_count] + hist[high_count : 2 * high_count])
        value_maps.append(hist[2 * high_count : 3 * high_count] + hist[3 * high_count :])

    chunk_rows = 8
    width = chunk_rows * LANES
    vec_row = lax.broadcasted_iota(jnp.int32, (16, width), 0)
    depth = (2 * days + 1) * members + 16
    sums = jnp.zeros((depth, members), F32)
    for first in range(0, high_count, chunk_rows):
        back = back_ref[:, first * LANES : first * LANES + width]
        back_wide = back.astype(F32)
        vectors = jnp.zeros((16, width), F32)
        for day in range(days):
            line = jnp.concatenate(
                [weight_maps[day][j : j + 1] for j in range(first, first + chunk_rows)], axis=1
            )
            part_high, part_low = terms(back_wide * line, 2)
            weighted[2 * day * members : (2 * day + 1) * members, :] = part_high
            weighted[(2 * day + 1) * members : (2 * day + 2) * members, :] = part_low
            line = jnp.concatenate(
                [value_maps[day][j : j + 1] for j in range(first, first + chunk_rows)], axis=1
            )
            line_high, line_low = terms(line, 2)
            vectors = jnp.where(vec_row == day, line_high.astype(F32), vectors)
            vectors = jnp.where(vec_row == day + 8, line_low.astype(F32), vectors)
        weighted[2 * days * members : (2 * days + 1) * members, :] = back
        weighted[(2 * days + 1) * members :, :] = vectors.astype(BF16)
        sums = sums + dot_16(weighted[...], back, NT)

    infos = [
        sums[2 * day * members : (2 * day + 1) * members]
        + sums[(2 * day + 1) * members : (2 * day + 2) * members]
        for day in range(days)
    ]
    turned = dot_high(jnp.concatenate(infos, axis=0), probe, NT)
    columns = [
        dot_high(probe, turned[day * members : (day + 1) * members]) for day in range(days)
    ]
    gram = sums[2 * days * members : (2 * days + 1) * members]
    tail = sums[(2 * days + 1) * members :]
    vector_rows = tail[:8] + tail[8:]
    vector_rows = jnp.concatenate([vector_rows, jnp.zeros((side - 8, members), F32)], axis=0)
    columns.append(dot_high(probe, vector_rows, NT) + extra)
    upper = jnp.concatenate(columns, axis=1)
    lower = jnp.concatenate([gram[:rank], gram[rank:]], axis=1)
    height = payload.shape[1]
    for i in range(space_count):
        start = i * height
        payload[i] = (
            upper[start : start + height] if start < rank else lower[start - rank : start - rank + height]
        )

    copies = [
        space_copy(step, payload.at[space_peer(step)[1]], held.at[step], send_sum, recv_sum)
        for step in range(1, space_count)
    ]
    for copy in copies:
        copy.start()
    added = payload[me]
    for step in range(1, space_count):
        copies[step - 1].wait()
        added = added + held[step]
    out_ref[me, time_index] = added
    copies = [
        pltpu.make_async_remote_copy(
            src_ref=out_ref.at[me, time_index],
            dst_ref=out_ref.at[me, time_index],
            send_sem=send_time.at[step],
            recv_sem=recv_time.at[step],
            device_id=time_peer(step),
            device_id_type=MESH,
        )
        for step in range(1, time_count)
    ]
    for copy in copies:
        copy.start()
    for copy in copies:
        copy.wait()
    copies = [
        space_copy(step, out_ref.at[me], out_ref.at[me], send_all, recv_all)
        for step in range(1, space_count)
    ]
    for copy in copies:
        copy.start()
    for copy in copies:
        copy.wait()


def eliminate(mats, rank, only_below):
    tile = (8, LANES)
    row = lax.broadcasted_iota(jnp.int32, tile, 0)
    count = rank // 8
    all_tiles = [[mat[8 * j : 8 * j + 8, :] for j in range(count)] for mat in mats]

    def spread_row(value, index):
        return jnp.broadcast_to(value[index : index + 1, :], tile)

    def spread_lane(value, index):
        return jnp.broadcast_to(value[:, index : index + 1], tile)

    for k in range(0, rank, 2):
        own, at = k // 8, k % 8
        for tiles in all_tiles:
            active = range(own, count) if only_below else range(count)
            col_a = {j: spread_lane(tiles[j], rank + k) for j in active}
            col_b = {j: spread_lane(tiles[j], rank + k + 1) for j in active}
            row_a, row_b = spread_row(tiles[own], at), spread_row(tiles[own], at + 1)
            a, b = spread_row(col_a[own], at), spread_row(col_b[own], at)
            c = spread_row(col_b[own], at + 1)
            scale = 1.0 / (a * c - b * b)
            new_a = (c * row_a - b * row_b) * scale
            new_b = (a * row_b - b * row_a) * scale
            if only_below:
                second = row_b - (b / a) * row_a
            for j in active:
                update = tiles[j] - col_a[j] * new_a - col_b[j] * new_b
                if j != own:
                    tiles[j] = update
                elif only_below:
                    tiles[j] = jnp.where(
                        row > at + 1, update, jnp.where(row == at + 1, second, tiles[j])
                    )
                else:
                    tiles[j] = jnp.where(
                        row == at, new_a, jnp.where(row == at + 1, new_b, update)
                    )
    return [jnp.concatenate(tiles, axis=0) for tiles in all_tiles]


def factor_rows(mat, rank, eye):
    pivots = jnp.sum(mat[:, rank : 2 * rank] * eye, axis=1, keepdims=True)
    return mat * lax.rsqrt(pivots)


def smooth_kernel(
    days_dev,
    pay_ref,
    probe_ref,
    scale_ref,
    back_hbm,
    mean_ref,
    spread_ref,
    aug_ref,
    low_ref,
    top_ref,
    back_ref,
    back_sem,
):
    load = pltpu.make_async_copy(back_hbm, back_ref, back_sem)
    load.start()
    space_count, time_count, height = pay_ref.shape[:3]
    rank, members = probe_ref.shape
    cells = back_ref.shape[1]
    days = time_count * days_dev
    stages = (days - 1).bit_length()
    reach = 1 << (stages - 1)
    rows = lax.broadcasted_iota(jnp.int32, (rank, rank), 0)
    eye = (rows == lax.broadcasted_iota(jnp.int32, (rank, rank), 1)).astype(F32)
    zero = jnp.zeros((rank, rank), F32)
    probe = scaled_rows(probe_ref, scale_ref)
    upper_count = rank // height
    gram_pair = jnp.concatenate(
        [pay_ref[s, 0] for s in range(upper_count, space_count)], axis=0
    )
    gram = jnp.concatenate([gram_pair[:, :members], gram_pair[:, members:]], axis=0)
    half = dot_high(probe, gram)
    core_gram = dot_high(half, probe, NT)
    reduced = eliminate([jnp.concatenate([zero, core_gram, eye, zero], axis=1)], rank, True)[0]
    lower_inv = factor_rows(reduced, rank, eye)[:, 2 * rank : 3 * rank]
    lower_probe = dot_high(lower_inv, probe)
    projected = dot_high(lower_inv, half)
    scale = scale_ref[...]
    prior = dot_high(projected * (scale * scale), projected, NT)

    def flat(column):
        return jnp.sum(eye * column, axis=0, keepdims=True)

    blocks = [
        jnp.concatenate([pay_ref[s, i] for s in range(upper_count)], axis=0)
        for i in range(time_count)
    ]
    side = days_dev * rank
    decay_col = []
    share = []
    for block in blocks:
        for i in range(days_dev):
            decay_col.append(block[:, side + days_dev + i : side + days_dev + i + 1])
            share.append(block[:, side + 2 * days_dev + i : side + 2 * days_dev + i + 1])
    decay_row = [flat(column) for column in decay_col]
    opening = decay_col[0] * prior * decay_row[0] + share[0] * prior
    pair = eliminate(
        [jnp.concatenate([zero, m, eye, zero], axis=1) for m in (prior, opening)], rank, False
    )
    prior_inv = pair[0][:, 2 * rank : 3 * rank]
    opening_inv = pair[1][:, 2 * rank : 3 * rank]
    cores = []
    infos = []
    for block in blocks:
        turned = dot_high(lower_inv, block)
        for i in range(days_dev):
            cores.append(turned[:, i * rank : (i + 1) * rank])
            infos.append(turned[:, side + i : side + i + 1])
    cores = dot_high(jnp.concatenate(cores, axis=0), lower_inv, NT)
    lane = lax.broadcasted_iota(jnp.int32, (rank, rank), 1)
    for t in range(days):
        rate = 1.0 / share[t]
        own = opening_inv if t == 0 else prior_inv * rate
        back = zero if t == 0 else -(prior_inv * decay_row[t]) * rate
        diagonal = own + cores[t * rank : (t + 1) * rank]
        ahead = zero
        if t + 1 < days:
            scaled = decay_col[t + 1] * prior_inv * (1.0 / share[t + 1])
            diagonal = diagonal + scaled * decay_row[t + 1]
            ahead = -scaled
        info = jnp.where(lane == 0, infos[t], 0.0)
        aug_ref[t] = jnp.concatenate([back, diagonal, ahead, info], axis=1)

    blank = jnp.zeros((reach, rank, LANES), F32)
    for ref in (low_ref, top_ref):
        ref[:reach] = blank
        ref[reach + days :] = blank
    wide = lax.broadcasted_iota(jnp.int32, (rank, LANES), 1)
    middle = (wide >= rank) & (wide < 2 * rank)
    last = wide >= 3 * rank

    def stage(index, _):
        distance = jnp.left_shift(1, index)
        mats = [aug_ref[t] for t in range(days)]
        solved = eliminate(mats, rank, False)
        for t in range(days):
            product = dot_terms_tn(aug_ref[t], solved[t])
            top = product[:rank]
            low = product[2 * rank : 3 * rank]
            top_ref[reach + t] = jnp.where(
                middle, pltpu.roll(top, rank, 1), jnp.where(wide >= 2 * rank, top, 0.0)
            )
            low_ref[reach + t] = jnp.where(
                middle,
                pltpu.roll(low, LANES - rank, 1),
                jnp.where((wide < rank) | last, low, 0.0),
            )
        for t in range(days):
            kept = jnp.where(middle | last, aug_ref[t], 0.0)
            aug_ref[t] = kept - low_ref[reach + t - distance] - top_ref[reach + t + distance]
        return _

    lax.fori_loop(0, stages, stage, 0)

    first = lax.axis_index("tm") * days_dev
    own = []
    for i in range(days_dev):
        mat = aug_ref[first + i]
        own.append(jnp.concatenate([eye, mat[:, rank:]], axis=1))
    own = [factor_rows(mat, rank, eye) for mat in eliminate(own, rank, True)]
    roots = jnp.concatenate([mat[:, :rank] for mat in own], axis=0)
    infos = [mat[:, 3 * rank : 3 * rank + 1] for mat in own]
    coefs = terms(dot_high(roots, lower_probe), 3)
    width = 8 * LANES
    load.wait()
    for start in range(0, cells, width):
        back = back_ref[:, start : start + width]
        field = dot_16(coefs[0], back) + dot_16(coefs[1], back) + dot_16(coefs[2], back)
        for i in range(days_dev):
            part = field[i * rank : (i + 1) * rank]
            mean_ref[i : i + 1, start : start + width] = jnp.sum(
                part * infos[i], axis=0, keepdims=True
            )
            spread_ref[i : i + 1, start : start + width] = jnp.sum(
                part * part, axis=0, keepdims=True
            )


VMEM = pl.BlockSpec(memory_space=pltpu.VMEM)
ANY = pl.BlockSpec(memory_space=pl.ANY)
PARAMS = pltpu.CompilerParams(vmem_limit_bytes=56 * 1024 * 1024)


def body(
    background, probe, member_scale, decay, inflation, obs_owner, obs_offset, obs_value, obs_weight
):
    members, rank = probe.shape
    cells = background.shape[0]
    days_dev = decay.shape[0]
    obs_dev = obs_offset.shape[1]
    space_count = lax.axis_size("space")
    time_count = lax.axis_size("tm")
    days = days_dev * time_count
    cap = 2 * obs_dev // space_count
    rows_owner = cap // LANES
    probe_rows = probe.T
    scale_row = member_scale[None, :]
    back = background.T
    slab = (space_count, 3 * days_dev * rows_owner, LANES)
    height = (rank + members // 2) // space_count
    part = (space_count, height, LANES)
    dma = pltpu.SemaphoreType.DMA
    summed = pl.pallas_call(
        functools.partial(gather_kernel, time_count, space_count, cap),
        out_shape=jax.ShapeDtypeStruct((space_count, time_count, height, LANES), F32),
        in_specs=[ANY] * 9,
        out_specs=VMEM,
        scratch_shapes=[
            pltpu.VMEM((days_dev, 1, obs_dev), jnp.int32),
            pltpu.VMEM((days_dev, obs_dev), jnp.int32),
            pltpu.VMEM((days_dev, obs_dev), F32),
            pltpu.VMEM((days_dev, obs_dev), F32),
            pltpu.VMEM((members, cells), BF16),
            pltpu.VMEM((rank, members), BF16),
            pltpu.VMEM((1, members), F32),
            pltpu.VMEM((days_dev, rank), F32),
            pltpu.VMEM((1, days_dev), F32),
            pltpu.VMEM(slab, F32),
            pltpu.VMEM(slab, F32),
            pltpu.VMEM(((2 * days_dev + 1) * members + 16, 8 * LANES), BF16),
            pltpu.VMEM((days_dev, 4 * (cells // LANES), LANES), F32),
            pltpu.VMEM(part, F32),
            pltpu.VMEM(part, F32),
            dma((9,)),
            dma((space_count,)),
            dma((space_count,)),
            dma((space_count,)),
            dma((space_count,)),
            dma((time_count,)),
            dma((time_count,)),
            dma((space_count,)),
            dma((space_count,)),
        ],
        compiler_params=pltpu.CompilerParams(
            collective_id=0, has_side_effects=True, vmem_limit_bytes=56 * 1024 * 1024
        ),
        name="gather",
    )(
        jnp.swapaxes(obs_owner, 1, 2),
        obs_offset,
        obs_value,
        obs_weight,
        back,
        probe_rows,
        scale_row,
        decay,
        inflation[None, :],
    )
    reach = 1 << ((days - 1).bit_length() - 1)
    return pl.pallas_call(
        functools.partial(smooth_kernel, days_dev),
        out_shape=[jax.ShapeDtypeStruct((days_dev, cells), F32)] * 2,
        in_specs=[VMEM] * 3 + [ANY],
        out_specs=[VMEM] * 2,
        scratch_shapes=[
            pltpu.VMEM((days, rank, LANES), F32),
            pltpu.VMEM((days + 2 * reach, rank, LANES), F32),
            pltpu.VMEM((days + 2 * reach, rank, LANES), F32),
            pltpu.VMEM((members, cells), BF16),
            pltpu.SemaphoreType.DMA,
        ],
        compiler_params=PARAMS,
        name="smoother",
    )(summed, probe_rows, scale_row, back)


def solution(mesh):
    return jax.shard_map(
        body,
        mesh=mesh,
        in_specs=(
            P("space", None),
            P(),
            P(),
            P("tm", None),
            P("tm"),
            P("tm", "space", None),
            P("tm", "space"),
            P("tm", "space"),
            P("tm", "space"),
        ),
        out_specs=(P("tm", "space"), P("tm", "space")),
        check_vma=False,
    )
```

```python
import functools

import jax
import jax.numpy as jnp
from jax import lax
from jax.experimental import pallas as pl
from jax.experimental.pallas import tpu as pltpu
from jax.sharding import PartitionSpec as P

HIGHEST = lax.Precision.HIGHEST
MESH = pl.DeviceIdType.MESH
F32 = jnp.float32
BF16 = jnp.bfloat16
LANES = 128
NT = (((1,), (1,)), ((), ()))
NN = (((1,), (0,)), ((), ()))
TN = (((0,), (0,)), ((), ()))


def dot_high(left, right, dims=NN):
    return lax.dot_general(left, right, dims, precision=HIGHEST, preferred_element_type=F32)


def dot_16(left, right, dims=NN):
    return lax.dot_general(left, right, dims, preferred_element_type=F32)


def terms(value, count):
    parts = []
    rest = value
    for step in range(count):
        part = rest.astype(BF16)
        parts.append(part)
        if step < count - 1:
            rest = rest - part.astype(F32)
    return parts


def dot_terms_tn(left, right):
    l1, l2, l3 = terms(left, 3)
    r1, r2, r3 = terms(right, 3)
    return dot_16(
        jnp.concatenate([l1, l1, l2, l2, l1, l3], axis=0),
        jnp.concatenate([r1, r2, r1, r2, r3, r1], axis=0),
        TN,
    )


def scaled_rows(probe_ref, scale_ref):
    scaled = (probe_ref[...].astype(F32) * scale_ref[...]).astype(BF16)
    return scaled.astype(F32)


def make_buckets(space_count, cap, owner_ref, offset_ref, value_ref, weight_ref, out_ref):
    days, count = offset_ref.shape
    chunks = count // LANES
    rows_owner = cap // LANES
    slot_rows = space_count * rows_owner
    before = lax.broadcasted_iota(jnp.int32, (LANES, LANES), 0)
    after = lax.broadcasted_iota(jnp.int32, (LANES, LANES), 1)
    earlier = (before < after).astype(F32).astype(BF16)
    ones = jnp.ones((LANES, LANES), BF16)
    owner_row = lax.broadcasted_iota(jnp.int32, (space_count, LANES), 0)
    for day in range(days):
        hits = []
        for chunk in range(chunks):
            own = owner_ref[day, :, chunk * LANES : (chunk + 1) * LANES]
            hits.append((owner_row == own).astype(F32))
        stacked = jnp.concatenate(hits, axis=0).astype(BF16)
        inside = dot_16(stacked, earlier)
        totals = dot_16(stacked, ones)
        base = (owner_row * cap).astype(F32)
        slots = []
        for chunk in range(chunks):
            part = slice(chunk * space_count, (chunk + 1) * space_count)
            place = hits[chunk] * (inside[part] + base)
            slots.append(jnp.sum(place, axis=0, keepdims=True))
            base = base + totals[part]
        slot = jnp.concatenate(slots, axis=1).astype(jnp.int32)
        slot_high = slot // LANES
        slot_low = slot - slot_high * LANES
        offset = offset_ref[day : day + 1, :]
        offset_high = offset // LANES
        pieces = terms(weight_ref[day : day + 1, :], 3) + terms(value_ref[day : day + 1, :], 3)
        pieces = [piece.astype(F32) for piece in pieces]
        pieces += [offset_high.astype(F32), (offset - offset_high * LANES).astype(F32)]
        in_row = lax.broadcasted_iota(jnp.int32, (slot_rows, count), 0) == slot_high
        left = jnp.concatenate(
            [jnp.where(in_row, piece, 0.0).astype(BF16) for piece in pieces], axis=0
        )
        right = (
            (lax.broadcasted_iota(jnp.int32, (LANES, count), 0) == slot_low)
            .astype(F32)
            .astype(BF16)
        )
        placed = dot_16(left, right, NT)
        cut = [placed[i * slot_rows : (i + 1) * slot_rows] for i in range(8)]
        whole = (cut[0] + cut[1] + cut[2], cut[3] + cut[4] + cut[5], cut[6] * LANES + cut[7])
        for kind in range(3):
            start = (kind * days + day) * rows_owner
            for owner in range(space_count):
                out_ref[owner, start : start + rows_owner, :] = whole[kind][
                    owner * rows_owner : (owner + 1) * rows_owner
                ]


def gather_kernel(
    time_count,
    space_count,
    cap,
    owner_hbm,
    offset_hbm,
    value_hbm,
    weight_hbm,
    back_hbm,
    probe_hbm,
    scale_hbm,
    decay_hbm,
    inflation_hbm,
    out_ref,
    owner_ref,
    offset_ref,
    value_ref,
    weight_ref,
    back_ref,
    probe_ref,
    scale_ref,
    decay_ref,
    inflation_ref,
    sent,
    got,
    weighted,
    hists,
    payload,
    held,
    local_sem,
    send_sem,
    recv_sem,
    send_sum,
    recv_sum,
    send_time,
    recv_time,
    send_all,
    recv_all,
):
    time_index = lax.axis_index("tm")
    me = lax.axis_index("space")
    days = offset_ref.shape[0]
    rows_owner = cap // LANES
    members, cells = back_ref.shape
    rank = probe_ref.shape[0]
    high_count = cells // LANES

    def space_peer(step):
        return (time_index, lax.rem(me + step, space_count))

    def time_peer(step):
        return (lax.rem(time_index + step, time_count), me)

    loads = [
        pltpu.make_async_copy(source, target, local_sem.at[i])
        for i, (source, target) in enumerate(
            (
                (owner_hbm, owner_ref),
                (offset_hbm, offset_ref),
                (value_hbm, value_ref),
                (weight_hbm, weight_ref),
                (back_hbm, back_ref),
                (probe_hbm, probe_ref),
                (scale_hbm, scale_ref),
                (decay_hbm, decay_ref),
                (inflation_hbm, inflation_ref),
            )
        )
    ]
    for load in loads:
        load.start()
    barrier = pltpu.get_barrier_semaphore()
    for step in range(1, space_count):
        pl.semaphore_signal(barrier, inc=1, device_id=space_peer(step), device_id_type=MESH)
    for step in range(1, time_count):
        pl.semaphore_signal(barrier, inc=1, device_id=time_peer(step), device_id_type=MESH)
    for load in loads[:4]:
        load.wait()
    make_buckets(space_count, cap, owner_ref, offset_ref, value_ref, weight_ref, sent)
    pl.semaphore_wait(barrier, space_count + time_count - 2)

    def space_copy(step, source, target, sends, receives):
        return pltpu.make_async_remote_copy(
            src_ref=source,
            dst_ref=target,
            send_sem=sends.at[step],
            recv_sem=receives.at[step],
            device_id=space_peer(step),
            device_id_type=MESH,
        )

    copies = [
        space_copy(step, sent.at[space_peer(step)[1]], got.at[step], send_sem, recv_sem)
        for step in range(1, space_count)
    ]
    for copy in copies:
        copy.start()
    for load in loads[4:]:
        load.wait()
    probe = scaled_rows(probe_ref, scale_ref)
    at_row = lax.broadcasted_iota(jnp.int32, (rank, rank), 0)
    at_lane = lax.broadcasted_iota(jnp.int32, (rank, rank), 1)
    side = LANES - days * rank
    side_lane = lax.broadcasted_iota(jnp.int32, (rank, side), 1)
    extra = jnp.zeros((rank, side), F32)
    for day in range(days):
        line = jnp.where(at_row == at_lane, decay_ref[day : day + 1, :], 0.0)
        column = jnp.sum(line, axis=1, keepdims=True)
        extra = jnp.where(side_lane == days + day, column, extra)
        share = inflation_ref[:, day : day + 1]
        extra = jnp.where(side_lane == 2 * days + day, share, extra)
    extra = extra * (me == 0).astype(F32)

    slots = rows_owner * LANES
    high_row = lax.broadcasted_iota(jnp.int32, (high_count, slots), 0)
    low_row = lax.broadcasted_iota(jnp.int32, (LANES, slots), 0)
    for step in range(space_count):
        if step > 0:
            copies[step - 1].wait()
            slab = got[step]
        else:
            slab = sent[me]
        for day in range(days):

            def rows(kind):
                start = (kind * days + day) * rows_owner
                return jnp.concatenate(
                    [slab[start + j : start + j + 1, :] for j in range(rows_owner)], axis=1
                )

            weight = rows(0)
            product = weight * rows(1)
            offset = rows(2).astype(jnp.int32)
            high = offset // LANES
            low = offset - high * LANES
            pieces = terms(weight, 2) + terms(product, 2)
            in_row = high_row == high
            left = jnp.concatenate(
                [jnp.where(in_row, piece.astype(F32), 0.0).astype(BF16) for piece in pieces],
                axis=0,
            )
            right = (low_row == low).astype(F32).astype(BF16)
            part = dot_16(left, right, NT)
            hists[day] = part if step == 0 else hists[day] + part
    weight_maps = []
    value_maps = []
    for day in range(days):
        hist = hists[day]
        weight_maps.append(hist[:high_count] + hist[high_count : 2 * high_count])
        value_maps.append(hist[2 * high_count : 3 * high_count] + hist[3 * high_count :])

    chunk_rows = 8
    width = chunk_rows * LANES
    vec_row = lax.broadcasted_iota(jnp.int32, (16, width), 0)
    depth = (2 * days + 1) * members + 16
    sums = jnp.zeros((depth, members), F32)
    for first in range(0, high_count, chunk_rows):
        back = back_ref[:, first * LANES : first * LANES + width]
        back_wide = back.astype(F32)
        vectors = jnp.zeros((16, width), F32)
        for day in range(days):
            line = jnp.concatenate(
                [weight_maps[day][j : j + 1] for j in range(first, first + chunk_rows)], axis=1
            )
            part_high, part_low = terms(back_wide * line, 2)
            weighted[2 * day * members : (2 * day + 1) * members, :] = part_high
            weighted[(2 * day + 1) * members : (2 * day + 2) * members, :] = part_low
            line = jnp.concatenate(
                [value_maps[day][j : j + 1] for j in range(first, first + chunk_rows)], axis=1
            )
            line_high, line_low = terms(line, 2)
            vectors = jnp.where(vec_row == day, line_high.astype(F32), vectors)
            vectors = jnp.where(vec_row == day + 8, line_low.astype(F32), vectors)
        weighted[2 * days * members : (2 * days + 1) * members, :] = back
        weighted[(2 * days + 1) * members :, :] = vectors.astype(BF16)
        sums = sums + dot_16(weighted[...], back, NT)

    infos = [
        sums[2 * day * members : (2 * day + 1) * members]
        + sums[(2 * day + 1) * members : (2 * day + 2) * members]
        for day in range(days)
    ]
    turned = dot_high(jnp.concatenate(infos, axis=0), probe, NT)
    columns = [
        dot_high(probe, turned[day * members : (day + 1) * members]) for day in range(days)
    ]
    gram = sums[2 * days * members : (2 * days + 1) * members]
    tail = sums[(2 * days + 1) * members :]
    vector_rows = tail[:8] + tail[8:]
    vector_rows = jnp.concatenate([vector_rows, jnp.zeros((side - 8, members), F32)], axis=0)
    columns.append(dot_high(probe, vector_rows, NT) + extra)
    upper = jnp.concatenate(columns, axis=1)
    lower = jnp.concatenate([gram[:rank], gram[rank:]], axis=1)
    height = payload.shape[1]
    for i in range(space_count):
        start = i * height
        payload[i] = (
            upper[start : start + height] if start < rank else lower[start - rank : start - rank + height]
        )

    copies = [
        space_copy(step, payload.at[space_peer(step)[1]], held.at[step], send_sum, recv_sum)
        for step in range(1, space_count)
    ]
    for copy in copies:
        copy.start()
    added = payload[me]
    for step in range(1, space_count):
        copies[step - 1].wait()
        added = added + held[step]
    out_ref[me, time_index] = added
    copies = [
        pltpu.make_async_remote_copy(
            src_ref=out_ref.at[me, time_index],
            dst_ref=out_ref.at[me, time_index],
            send_sem=send_time.at[step],
            recv_sem=recv_time.at[step],
            device_id=time_peer(step),
            device_id_type=MESH,
        )
        for step in range(1, time_count)
    ]
    for copy in copies:
        copy.start()
    for copy in copies:
        copy.wait()
    copies = [
        space_copy(step, out_ref.at[me], out_ref.at[me], send_all, recv_all)
        for step in range(1, space_count)
    ]
    for copy in copies:
        copy.start()
    for copy in copies:
        copy.wait()


def eliminate(mats, rank, only_below):
    tile = (8, LANES)
    row = lax.broadcasted_iota(jnp.int32, tile, 0)
    count = rank // 8
    all_tiles = [[mat[8 * j : 8 * j + 8, :] for j in range(count)] for mat in mats]

    def spread_row(value, index):
        return jnp.broadcast_to(value[index : index + 1, :], tile)

    def spread_lane(value, index):
        return jnp.broadcast_to(value[:, index : index + 1], tile)

    for k in range(0, rank, 2):
        own, at = k // 8, k % 8
        for tiles in all_tiles:
            active = range(own, count) if only_below else range(count)
            col_a = {j: spread_lane(tiles[j], rank + k) for j in active}
            col_b = {j: spread_lane(tiles[j], rank + k + 1) for j in active}
            row_a, row_b = spread_row(tiles[own], at), spread_row(tiles[own], at + 1)
            a, b = spread_row(col_a[own], at), spread_row(col_b[own], at)
            c = spread_row(col_b[own], at + 1)
            scale = 1.0 / (a * c - b * b)
            new_a = (c * row_a - b * row_b) * scale
            new_b = (a * row_b - b * row_a) * scale
            if only_below:
                second = row_b - (b / a) * row_a
            for j in active:
                update = tiles[j] - col_a[j] * new_a - col_b[j] * new_b
                if j != own:
                    tiles[j] = update
                elif only_below:
                    tiles[j] = jnp.where(
                        row > at + 1, update, jnp.where(row == at + 1, second, tiles[j])
                    )
                else:
                    tiles[j] = jnp.where(
                        row == at, new_a, jnp.where(row == at + 1, new_b, update)
                    )
    return [jnp.concatenate(tiles, axis=0) for tiles in all_tiles]


def factor_rows(mat, rank, eye):
    pivots = jnp.sum(mat[:, rank : 2 * rank] * eye, axis=1, keepdims=True)
    return mat * lax.rsqrt(pivots)


def smooth_kernel(
    days_dev,
    pay_ref,
    probe_ref,
    scale_ref,
    back_hbm,
    mean_ref,
    spread_ref,
    aug_ref,
    low_ref,
    top_ref,
    back_ref,
    back_sem,
):
    load = pltpu.make_async_copy(back_hbm, back_ref, back_sem)
    load.start()
    space_count, time_count, height = pay_ref.shape[:3]
    rank, members = probe_ref.shape
    cells = back_ref.shape[1]
    days = time_count * days_dev
    stages = (days - 1).bit_length()
    reach = 1 << (stages - 1)
    rows = lax.broadcasted_iota(jnp.int32, (rank, rank), 0)
    eye = (rows == lax.broadcasted_iota(jnp.int32, (rank, rank), 1)).astype(F32)
    zero = jnp.zeros((rank, rank), F32)
    probe = scaled_rows(probe_ref, scale_ref)
    upper_count = rank // height
    gram_pair = jnp.concatenate(
        [pay_ref[s, 0] for s in range(upper_count, space_count)], axis=0
    )
    gram = jnp.concatenate([gram_pair[:, :members], gram_pair[:, members:]], axis=0)
    half = dot_high(probe, gram)
    core_gram = dot_high(half, probe, NT)
    reduced = eliminate([jnp.concatenate([zero, core_gram, eye, zero], axis=1)], rank, True)[0]
    lower_inv = factor_rows(reduced, rank, eye)[:, 2 * rank : 3 * rank]
    lower_probe = dot_high(lower_inv, probe)
    projected = dot_high(lower_inv, half)
    scale = scale_ref[...]
    prior = dot_high(projected * (scale * scale), projected, NT)

    def flat(column):
        return jnp.sum(eye * column, axis=0, keepdims=True)

    blocks = [
        jnp.concatenate([pay_ref[s, i] for s in range(upper_count)], axis=0)
        for i in range(time_count)
    ]
    side = days_dev * rank
    decay_col = []
    share = []
    for block in blocks:
        for i in range(days_dev):
            decay_col.append(block[:, side + days_dev + i : side + days_dev + i + 1])
            share.append(block[:, side + 2 * days_dev + i : side + 2 * days_dev + i + 1])
    decay_row = [flat(column) for column in decay_col]
    opening = decay_col[0] * prior * decay_row[0] + share[0] * prior
    pair = eliminate(
        [jnp.concatenate([zero, m, eye, zero], axis=1) for m in (prior, opening)], rank, False
    )
    prior_inv = pair[0][:, 2 * rank : 3 * rank]
    opening_inv = pair[1][:, 2 * rank : 3 * rank]
    cores = []
    infos = []
    for block in blocks:
        turned = dot_high(lower_inv, block)
        for i in range(days_dev):
            cores.append(turned[:, i * rank : (i + 1) * rank])
            infos.append(turned[:, side + i : side + i + 1])
    cores = dot_high(jnp.concatenate(cores, axis=0), lower_inv, NT)
    lane = lax.broadcasted_iota(jnp.int32, (rank, rank), 1)
    for t in range(days):
        rate = 1.0 / share[t]
        own = opening_inv if t == 0 else prior_inv * rate
        back = zero if t == 0 else -(prior_inv * decay_row[t]) * rate
        diagonal = own + cores[t * rank : (t + 1) * rank]
        ahead = zero
        if t + 1 < days:
            scaled = decay_col[t + 1] * prior_inv * (1.0 / share[t + 1])
            diagonal = diagonal + scaled * decay_row[t + 1]
            ahead = -scaled
        info = jnp.where(lane == 0, infos[t], 0.0)
        aug_ref[t] = jnp.concatenate([back, diagonal, ahead, info], axis=1)

    blank = jnp.zeros((reach, rank, LANES), F32)
    for ref in (low_ref, top_ref):
        ref[:reach] = blank
        ref[reach + days :] = blank
    wide = lax.broadcasted_iota(jnp.int32, (rank, LANES), 1)
    middle = (wide >= rank) & (wide < 2 * rank)
    last = wide >= 3 * rank

    def stage(index, _):
        distance = jnp.left_shift(1, index)
        mats = [aug_ref[t] for t in range(days)]
        halves = [factor_rows(mat, rank, eye) for mat in eliminate(mats, rank, True)]
        for t in range(days):
            product = dot_terms_tn(halves[t], halves[t])
            top = product[:rank]
            low = product[2 * rank : 3 * rank]
            top_ref[reach + t] = jnp.where(
                middle, pltpu.roll(top, rank, 1), jnp.where(wide >= 2 * rank, top, 0.0)
            )
            low_ref[reach + t] = jnp.where(
                middle,
                pltpu.roll(low, LANES - rank, 1),
                jnp.where((wide < rank) | last, low, 0.0),
            )
        for t in range(days):
            kept = jnp.where(middle | last, aug_ref[t], 0.0)
            aug_ref[t] = kept - low_ref[reach + t - distance] - top_ref[reach + t + distance]
        return _

    lax.fori_loop(0, stages, stage, 0)

    first = lax.axis_index("tm") * days_dev
    own = []
    for i in range(days_dev):
        mat = aug_ref[first + i]
        own.append(jnp.concatenate([eye, mat[:, rank:]], axis=1))
    own = [factor_rows(mat, rank, eye) for mat in eliminate(own, rank, True)]
    roots = jnp.concatenate([mat[:, :rank] for mat in own], axis=0)
    infos = [mat[:, 3 * rank : 3 * rank + 1] for mat in own]
    coefs = terms(dot_high(roots, lower_probe), 3)
    width = 8 * LANES
    load.wait()
    for start in range(0, cells, width):
        back = back_ref[:, start : start + width]
        field = dot_16(coefs[0], back) + dot_16(coefs[1], back) + dot_16(coefs[2], back)
        for i in range(days_dev):
            part = field[i * rank : (i + 1) * rank]
            mean_ref[i : i + 1, start : start + width] = jnp.sum(
                part * infos[i], axis=0, keepdims=True
            )
            spread_ref[i : i + 1, start : start + width] = jnp.sum(
                part * part, axis=0, keepdims=True
            )


VMEM = pl.BlockSpec(memory_space=pltpu.VMEM)
ANY = pl.BlockSpec(memory_space=pl.ANY)
PARAMS = pltpu.CompilerParams(vmem_limit_bytes=56 * 1024 * 1024)


def body(
    background, probe, member_scale, decay, inflation, obs_owner, obs_offset, obs_value, obs_weight
):
    members, rank = probe.shape
    cells = background.shape[0]
    days_dev = decay.shape[0]
    obs_dev = obs_offset.shape[1]
    space_count = lax.axis_size("space")
    time_count = lax.axis_size("tm")
    days = days_dev * time_count
    cap = 2 * obs_dev // space_count
    rows_owner = cap // LANES
    probe_rows = probe.T
    scale_row = member_scale[None, :]
    back = background.T
    slab = (space_count, 3 * days_dev * rows_owner, LANES)
    height = (rank + members // 2) // space_count
    part = (space_count, height, LANES)
    dma = pltpu.SemaphoreType.DMA
    summed = pl.pallas_call(
        functools.partial(gather_kernel, time_count, space_count, cap),
        out_shape=jax.ShapeDtypeStruct((space_count, time_count, height, LANES), F32),
        in_specs=[ANY] * 9,
        out_specs=VMEM,
        scratch_shapes=[
            pltpu.VMEM((days_dev, 1, obs_dev), jnp.int32),
            pltpu.VMEM((days_dev, obs_dev), jnp.int32),
            pltpu.VMEM((days_dev, obs_dev), F32),
            pltpu.VMEM((days_dev, obs_dev), F32),
            pltpu.VMEM((members, cells), BF16),
            pltpu.VMEM((rank, members), BF16),
            pltpu.VMEM((1, members), F32),
            pltpu.VMEM((days_dev, rank), F32),
            pltpu.VMEM((1, days_dev), F32),
            pltpu.VMEM(slab, F32),
            pltpu.VMEM(slab, F32),
            pltpu.VMEM(((2 * days_dev + 1) * members + 16, 8 * LANES), BF16),
            pltpu.VMEM((days_dev, 4 * (cells // LANES), LANES), F32),
            pltpu.VMEM(part, F32),
            pltpu.VMEM(part, F32),
            dma((9,)),
            dma((space_count,)),
            dma((space_count,)),
            dma((space_count,)),
            dma((space_count,)),
            dma((time_count,)),
            dma((time_count,)),
            dma((space_count,)),
            dma((space_count,)),
        ],
        compiler_params=pltpu.CompilerParams(
            collective_id=0, has_side_effects=True, vmem_limit_bytes=56 * 1024 * 1024
        ),
        name="gather",
    )(
        jnp.swapaxes(obs_owner, 1, 2),
        obs_offset,
        obs_value,
        obs_weight,
        back,
        probe_rows,
        scale_row,
        decay,
        inflation[None, :],
    )
    reach = 1 << ((days - 1).bit_length() - 1)
    return pl.pallas_call(
        functools.partial(smooth_kernel, days_dev),
        out_shape=[jax.ShapeDtypeStruct((days_dev, cells), F32)] * 2,
        in_specs=[VMEM] * 3 + [ANY],
        out_specs=[VMEM] * 2,
        scratch_shapes=[
            pltpu.VMEM((days, rank, LANES), F32),
            pltpu.VMEM((days + 2 * reach, rank, LANES), F32),
            pltpu.VMEM((days + 2 * reach, rank, LANES), F32),
            pltpu.VMEM((members, cells), BF16),
            pltpu.SemaphoreType.DMA,
        ],
        compiler_params=PARAMS,
        name="smoother",
    )(summed, probe_rows, scale_row, back)


def solution(mesh):
    return jax.shard_map(
        body,
        mesh=mesh,
        in_specs=(
            P("space", None),
            P(),
            P(),
            P("tm", None),
            P("tm"),
            P("tm", "space", None),
            P("tm", "space"),
            P("tm", "space"),
            P("tm", "space"),
        ),
        out_specs=(P("tm", "space"), P("tm", "space")),
        check_vma=False,
    )
```
